512 devices in a mesh: aux: 64 (over x, z), pair: 8 (over y, core).
Axes of the slice: x: 4, y: 4, z: 16, core: 2. Of those that a mesh axis runs over, the one named last changes fastest.
Arguments:
- three_center: bfloat16 [512, 64, 1024], P('aux', 'pair'), may hold values from -6 to 6
- tile_live: int32 [64, 64], P('aux', 'pair'), may hold values from 0 to 1
- pair_atoms: int32 [64], replicated, may hold values from 0 to 63, each once
- green_occ: bfloat16 [256, 256], replicated, may hold values from -0.375 to 0.375
- green_vir: bfloat16 [256, 256], replicated, may hold values from -0.375 to 0.375
- screened: bfloat16 [512, 40], P('aux'), may hold values from -1 to 1
Outputs:
- polarizability: float32 [512, 40], P('aux', 'pair')
- self_energy: float32 [64, 1024], P('pair')
The draws below stay inside these ranges and needn't reach their ends.
Inputs may be any that keep to these rules, and one draw needn't show every extreme that they name: `pair_atoms`: a permutation of the 64 atom pairs.
All inputs are finite; a program needn't handle non-finite values.
Results may differ from the reference program's by a relative error of at most 0.0043.
Values may be sent and summed in bfloat16 or wider, within the bound.
A program may use at most 64 MiB of HBM per device.

```python
import jax
import jax.numpy as jnp
from jax import lax

OA = 32
NAT = 8
AUX_DEV = 8
REACH = 2
NORB = 256
PAIR = 1024
NPT = 64
AUX_BLOCKS = 64
NAUX = 512
WIN = 40


def draw_tile_live(key, part):
    key_rows = jax.random.fold_in(key, 11)
    key_cells = jax.random.fold_in(key, 23)
    level = jax.random.randint(key_rows, (AUX_BLOCKS, 1), 1, 5)
    cells = jax.random.randint(key_cells, (AUX_BLOCKS, NPT), 0, 4)
    return (cells < level).astype(jnp.int32)


def shard_levels(own_key, dims, pieces, low, largest):
    def one(position, blocks):
        heights = jax.random.uniform(jax.random.fold_in(jax.random.fold_in(own_key, 6), position), (blocks,), jnp.float32, low / len(pieces), largest / len(pieces))
        return jnp.repeat(jnp.exp(heights), dims[position] // blocks).reshape((-1,) + (1,) * (len(dims) - position - 1))

    factor_of = one(*pieces[0])
    for cut in pieces[1:]:
        factor_of = factor_of * one(*cut)
    return factor_of


def centred(own_key, shape, scale, limit, split=(), kind=jnp.bfloat16):
    entries = jax.random.normal(own_key, shape, jnp.float32) * scale
    if len(split) > 0:
        entries = shard_levels(own_key, shape, split, -0.22, 0.18) * entries
    return jnp.clip(entries, min=-limit, max=limit).astype(kind)


def setup_inputs(seed: int = 0) -> dict:
    key_of = jax.random.split(jax.random.key(seed), 7)
    return {
        "three_center": centred(key_of[0], (NAUX, NPT, PAIR), 1.0, 6.0, ((0, 64), (1, 8))),
        "tile_live": draw_tile_live(jax.random.fold_in(key_of[6], 71), 0),
        "pair_atoms": jax.random.permutation(key_of[2], NPT).astype(jnp.int32),
        "green_occ": centred(key_of[3], (NORB, NORB), NORB ** -0.5, 0.375),
        "green_vir": centred(key_of[4], (NORB, NORB), NORB ** -0.5, 0.375),
        "screened": centred(key_of[5], (NAUX, WIN), WIN ** -0.5, 1.0, ((0, 64),)),
    }


def rounded(values):
    return lax.optimization_barrier(values.astype(jnp.bfloat16)).astype(jnp.float32)


def tiles_to_matrix(tile_data, inverse):
    tile_rows = tile_data.shape[0]
    ordered = jnp.take(tile_data, inverse, axis=1)
    reshaped = ordered.reshape(tile_rows, NAT, NAT, OA, OA)
    return jnp.transpose(reshaped, (0, 1, 3, 2, 4)).reshape(tile_rows, NAT * OA, NAT * OA)


def matrix_to_tiles(matrix, pair_atoms):
    tile_rows = matrix.shape[0]
    reshaped = matrix.reshape(tile_rows, NAT, OA, NAT, OA)
    ordered = jnp.transpose(reshaped, (0, 1, 3, 2, 4)).reshape(tile_rows, NAT * NAT, OA * OA)
    return jnp.take(ordered, pair_atoms, axis=1)


def reference(three_center, tile_live, pair_atoms, green_occ, green_vir, screened):
    aux_total = three_center.shape[0]
    block_count = aux_total // AUX_DEV
    live_rows = jnp.repeat(tile_live, AUX_DEV, axis=0).astype(jnp.bfloat16)
    masked = three_center * live_rows[:, :, None]
    inverse = jnp.argsort(pair_atoms).astype(jnp.int32)
    first_atom = pair_atoms // NAT
    second_atom = pair_atoms % NAT
    margin_rows = REACH * AUX_DEV
    padded = jnp.pad(masked, ((margin_rows, margin_rows), (0, 0), (0, 0)))
    occ_full = green_occ.astype(jnp.float32)
    vir_full = green_vir.astype(jnp.float32)
    chi_scale = 1.0 / (OA * NAT)
    sigma_scale = 1.0 / (aux_total * NAT * OA * NAT) ** 0.5

    def one_block(block_index):
        row_start = block_index * AUX_DEV
        own_rows = lax.dynamic_slice_in_dim(masked, row_start, AUX_DEV, 0)
        window = lax.dynamic_slice_in_dim(padded, row_start, WIN, 0)
        orbital_form = tiles_to_matrix(own_rows, inverse).astype(jnp.float32)
        left_half = rounded(jnp.einsum("lu,plm->pum", occ_full, orbital_form))
        full_form = rounded(jnp.einsum("pum,mv->puv", left_half, vir_full))
        products = matrix_to_tiles(full_form, pair_atoms)
        window_float = window.astype(jnp.float32)
        chi_block = jnp.einsum("pke,qke->pq", products, window_float) * chi_scale
        coupling = lax.dynamic_slice_in_dim(screened, row_start, AUX_DEV, 0).astype(jnp.float32)
        mixed_tiles = jnp.einsum("qw,wke->qke", coupling, window_float).astype(jnp.bfloat16)
        return chi_block, mixed_tiles

    chi_blocks, mixed_blocks = lax.map(one_block, jnp.arange(block_count, dtype=jnp.int32))
    polarizability = chi_blocks.reshape(aux_total, WIN)
    mixed_all = mixed_blocks.reshape(aux_total, NPT, OA * OA)
    occ_rows = jnp.take(occ_full.reshape(NAT, OA, NAT * OA), second_atom, axis=0)

    def accumulate(running, block_index):
        row_start = block_index * AUX_DEV
        own_rows = lax.dynamic_slice_in_dim(masked, row_start, AUX_DEV, 0)
        orbital_form = tiles_to_matrix(own_rows, inverse).astype(jnp.float32)
        mixed_tiles = lax.dynamic_slice_in_dim(mixed_all, row_start, AUX_DEV, 0).astype(jnp.float32)
        mixed_tiles = mixed_tiles.reshape(AUX_DEV, NPT, OA, OA)
        scaled_rows = rounded(jnp.einsum("qkml,kls->qkms", mixed_tiles, occ_rows))
        return running + jnp.einsum("qkms,qsn->kmn", scaled_rows, orbital_form), None

    start_sum = jnp.zeros((NPT, OA, NAT * OA), jnp.float32)
    term_sums, unused = lax.scan(accumulate, start_sum, jnp.arange(block_count, dtype=jnp.int32))
    atom_onehot = (first_atom[:, None] == jnp.arange(NAT, dtype=jnp.int32)[None, :]).astype(jnp.float32)
    by_atom = jnp.einsum("ka,kmn->amn", atom_onehot, term_sums, precision=lax.Precision.HIGHEST)
    self_energy = matrix_to_tiles(by_atom.reshape(1, NAT * OA, NAT * OA), pair_atoms)[0] * (-sigma_scale)
    return polarizability, self_energy
```

```python
import functools
import math

import jax
import jax.numpy as jnp
from jax import lax
from jax.experimental import pallas as pl
from jax.experimental.pallas import tpu as pltpu
from jax.sharding import PartitionSpec as P

MESH = pl.DeviceIdType.MESH
OA = 32
NAT = 8
REACH = 2
NX = 4
NZ = 16
F32 = jnp.float32
BF16 = jnp.bfloat16


def dot(a, b, dims=((1,), (0,))):
    return lax.dot_general(a, b, (dims, ((), ())), preferred_element_type=F32)


def iota(shape, dim):
    return lax.broadcasted_iota(jnp.int32, shape, dim)


def exchange_groups(parts):
    x0, x1, x2, x3 = parts
    lane = iota(x0.shape, 1)
    low = lane < 64
    even = (lane & 32) == 0
    y0 = jnp.where(low, x0, pltpu.roll(x2, 64, 1))
    y2 = jnp.where(low, pltpu.roll(x0, 64, 1), x2)
    y1 = jnp.where(low, x1, pltpu.roll(x3, 64, 1))
    y3 = jnp.where(low, pltpu.roll(x1, 64, 1), x3)
    z0 = jnp.where(even, y0, pltpu.roll(y1, 32, 1))
    z1 = jnp.where(even, pltpu.roll(y0, 96, 1), y1)
    z2 = jnp.where(even, y2, pltpu.roll(y3, 32, 1))
    z3 = jnp.where(even, pltpu.roll(y2, 96, 1), y3)
    return z0, z1, z2, z3


def to_matrix(tiles):
    cols = [tiles[:, g * 128 : (g + 1) * 128].reshape(2, 4, 8, 128) for g in range(8)]
    parts = [
        jnp.concatenate([c[:, bl] for c in cols], axis=0).reshape(128, 128) for bl in range(4)
    ]
    out = [z.reshape(8, 2, 8, 128) for z in exchange_groups(parts)]
    halves = [
        jnp.stack([z[:, bh] for z in out], axis=1).reshape(256, 128) for bh in range(2)
    ]
    return jnp.concatenate(halves, axis=1)


def to_tiles(matrix):
    halves = [matrix[:, bh * 128 : (bh + 1) * 128].reshape(8, 4, 8, 128) for bh in range(2)]
    parts = [
        jnp.stack([h[:, r] for h in halves], axis=1).reshape(128, 128) for r in range(4)
    ]
    out = [z.reshape(8, 2, 8, 128) for z in exchange_groups(parts)]
    cols = [
        jnp.stack([z[g] for z in out], axis=1).reshape(64, 128) for g in range(8)
    ]
    return jnp.concatenate(cols, axis=1)


def rows64(value):
    return value.astype(F32).reshape(64, value.shape[-1])


def kernel(
    n_aux,
    n_pair,
    tc_hbm,
    live_hbm,
    atoms_hbm,
    occ_hbm,
    vir_hbm,
    scr_hbm,
    pol_ref,
    self_ref,
    tc,
    live,
    atoms,
    occ,
    vir,
    scr,
    win,
    mt,
    zo,
    zt,
    vo,
    vt,
    xo,
    xr,
    chi,
    yo,
    yr,
    ar,
    fin,
    in_sem,
    s_win,
    r_win,
    s_m,
    r_m,
    s_z,
    r_z,
    s_v,
    r_v,
    s_x,
    r_x,
    s_c,
    r_c,
    s_y,
    r_y,
    s_a,
    r_a,
    s_f,
    r_f,
):
    a_me = lax.axis_index("aux")
    p_me = lax.axis_index("pair")
    x_me, z_me = a_me // NZ, a_me % NZ
    zh_me, par_me = z_me // 2, z_me % 2
    j_me = x_me * 2 + par_me

    loads = [
        pltpu.make_async_copy(src, dst, in_sem.at[i])
        for i, (src, dst) in enumerate(
            (
                (tc_hbm, tc),
                (live_hbm, live),
                (atoms_hbm, atoms),
                (occ_hbm, occ),
                (vir_hbm, vir),
                (scr_hbm, scr),
            )
        )
    ]
    for c in loads:
        c.start()

    def by_pair(step):
        q = lax.rem(p_me + step, n_pair)
        return q, (a_me, q)

    def by_group(step):
        j = lax.rem(j_me + step, 8)
        return j, ((j // 2) * NZ + zh_me * 2 + lax.rem(j, 2), p_me)

    def by_zh(step):
        h = lax.rem(zh_me + step, 8)
        return h, (x_me * NZ + h * 2 + par_me, p_me)

    offsets = (1, -1, 2, -2)

    def by_window(d):
        return (lax.rem(a_me + d + n_aux, n_aux), p_me)

    barrier = pltpu.get_barrier_semaphore()
    for d in offsets:
        pl.semaphore_signal(barrier, inc=1, device_id=by_window(d), device_id_type=MESH)
    for step in range(1, 8):
        for peer in (by_pair, by_group, by_zh):
            pl.semaphore_signal(barrier, inc=1, device_id=peer(step)[1], device_id_type=MESH)

    def remote(src, dst, send, recv, device):
        return pltpu.make_async_remote_copy(
            src_ref=src,
            dst_ref=dst,
            send_sem=send,
            recv_sem=recv,
            device_id=device,
            device_id_type=MESH,
        )

    def exchange(peer, me, source, dest, send, recv):
        copies = []
        for step in range(1, 8):
            there, device = peer(step)
            src = source(there)
            copies.append(remote(src, dest.at[me], send.at[step - 1], recv.at[step - 1], device))
        for c in copies:
            c.start()
        return copies

    loads[0].wait()
    loads[1].wait()
    eye8 = iota((8, 8), 0) == iota((8, 8), 1)
    live_col = jnp.sum(
        jnp.where(eye8, jnp.broadcast_to(live[...].astype(F32), (8, 8)), 0.0), axis=1, keepdims=True
    )
    win[REACH] = (tc[...].astype(F32) * live_col[None]).astype(BF16)

    pl.semaphore_wait(barrier, 25)
    started = []
    window_copies = {}
    for i, d in enumerate(offsets):
        c = remote(win.at[REACH], win.at[REACH - d], s_win.at[i], r_win.at[i], by_window(d))
        c.start()
        window_copies[REACH - d] = c
        started.append(c)
    m_copies = exchange(by_pair, p_me, lambda q: win.at[REACH, q], mt, s_m, r_m)
    started += m_copies
    mt[p_me] = win[REACH, p_me]

    for c in loads[2:]:
        c.wait()
    new = iota((256, 256), 0)
    old = iota((256, 256), 1)
    perm = jnp.where((new % 8) * 32 + new // 8 == old, 1.0, 0.0).astype(BF16)
    occ_cols = dot(occ[...], perm, ((1,), (1,))).astype(BF16)
    occ_both = dot(perm, occ_cols).astype(BF16)
    atom_row = atoms[...]
    place = iota((64, 64), 0)
    pick = jnp.where((place % 8) * 8 + place // 8 == atom_row, 1.0, 0.0).astype(BF16)
    eye64 = iota((64, 64), 0) == iota((64, 64), 1)
    atom_col = jnp.sum(
        jnp.where(eye64, jnp.broadcast_to(atom_row.astype(F32), (64, 64)), 0.0), axis=1, keepdims=True
    ).astype(jnp.int32)
    spot = iota((64, 64), 1)
    put = jnp.where((spot % 8) * 8 + spot // 8 == atom_col, 1.0, 0.0).astype(BF16)
    wide = jnp.broadcast_to(scr[...].astype(F32)[:, None, :], (8, 8, 40)).reshape(64, 40).astype(BF16)
    same_tile = (iota((64, 64), 0) % 8) == (iota((64, 64), 1) % 8)
    couple = []
    for slot in range(5):
        spread = jnp.where(iota((40, 64), 0) == slot * 8 + iota((40, 64), 1) // 8, 1.0, 0.0)
        block = a_me + slot - REACH
        inside = jnp.logical_and(block >= 0, block < n_aux)
        keep = jnp.logical_and(same_tile, inside)
        couple.append(jnp.where(keep, dot(wide, spread.astype(BF16)), 0.0).astype(BF16))

    for c in m_copies:
        c.wait_recv()
    form = to_matrix(dot(pick, rows64(mt[...]).astype(BF16))).astype(BF16)
    left = dot(occ_both, form, ((0,), (0,))).astype(BF16)
    product = dot(left, vir[...])
    z_tiles = dot(put, to_tiles(product).astype(BF16))
    zo[...] = z_tiles.reshape(8, 8, 1024).astype(BF16)
    z_copies = exchange(by_pair, p_me, lambda q: zo.at[q], zt, s_z, r_z)
    started += z_copies
    zt[p_me] = zo[p_me]

    mixed = dot(couple[2], rows64(win[2]).astype(BF16))
    for slot in (1, 3, 0, 4):
        window_copies[slot].wait_recv()
        mixed += dot(couple[slot], rows64(win[slot]).astype(BF16))
    vo[...] = mixed.reshape(8, 8, 1024).astype(BF16)
    v_copies = exchange(by_pair, p_me, lambda q: vo.at[q], vt, s_v, r_v)
    started += v_copies
    vt[p_me] = vo[p_me]

    for c in z_copies:
        c.wait_recv()
    z_rows = rows64(zt[...]).astype(BF16)
    chi_total = jnp.zeros((8, 128), F32)
    for slot in range(5):
        terms = dot(z_rows, rows64(win[slot]).astype(BF16), ((1,), (1,)))
        block = a_me + slot - REACH
        inside = jnp.logical_and(block >= 0, block < n_aux)
        keep = jnp.logical_and(same_tile, inside)
        terms = jnp.sum(jnp.where(keep, terms, 0.0).reshape(8, 8, 64), axis=1)
        gather = jnp.where(iota((64, 128), 1) == slot * 8 + iota((64, 128), 0) // 8, 1.0, 0.0)
        chi_total += jnp.dot(terms, gather, precision=lax.Precision.HIGHEST, preferred_element_type=F32)
    chi[p_me] = chi_total * (1.0 / (OA * NAT))
    c_copies = exchange(by_pair, p_me, lambda q: chi.at[p_me], chi, s_c, r_c)
    started += c_copies

    for c in v_copies:
        c.wait_recv()
    v_form = to_matrix(dot(pick, rows64(vt[...]).astype(BF16))).astype(BF16)
    scaled = dot(v_form, occ_cols).astype(BF16)
    energy = dot(scaled, form)
    xo[...] = dot(put, to_tiles(energy).astype(BF16)).reshape(8, 8, 1024).astype(BF16)
    x_copies = exchange(by_pair, p_me, lambda q: xo.at[q], xr, s_x, r_x)
    started += x_copies
    xr[p_me] = xo[p_me]

    for c in c_copies:
        c.wait_recv()
    chi_sum = jnp.sum(chi[...], axis=0)
    turned = pltpu.roll(chi_sum, lax.rem(128 - 5 * p_me, 128), 1)
    pol_ref[...] = turned[:, :5]

    for c in x_copies:
        c.wait_recv()
    block_sum = jnp.sum(xr[...].astype(F32), axis=0)
    for j in range(8):
        yo[j] = block_sum[:, j * 128 : (j + 1) * 128]
    y_copies = exchange(by_group, j_me, lambda j: yo.at[j], yr, s_y, r_y)
    started += y_copies
    yr[j_me] = yo[j_me]
    for c in y_copies:
        c.wait_recv()
    ar[zh_me] = jnp.sum(yr[...], axis=0)
    a_copies = exchange(by_zh, zh_me, lambda h: ar.at[zh_me], ar, s_a, r_a)
    started += a_copies
    for c in a_copies:
        c.wait_recv()
    scale = -1.0 / math.sqrt(n_aux * 8 * NAT * OA * NAT)
    fin[j_me] = jnp.sum(ar[...], axis=0) * scale
    f_copies = exchange(by_group, j_me, lambda j: fin.at[j_me], fin, s_f, r_f)
    started += f_copies
    for c in f_copies:
        c.wait_recv()
    for j in range(8):
        self_ref[:, j * 128 : (j + 1) * 128] = fin[j]
    for c in started:
        c.wait_send()


def solution(mesh):
    n_aux, n_pair = mesh.shape["aux"], mesh.shape["pair"]

    def per_device(three_center, tile_live, pair_atoms, green_occ, green_vir, screened):
        tiles = pltpu.VMEM((8, 8, 1024), BF16)
        pieces = pltpu.VMEM((8, 8, 128), F32)
        sems = pltpu.SemaphoreType.DMA((7,))
        return pl.pallas_call(
            functools.partial(kernel, n_aux, n_pair),
            out_shape=(
                jax.ShapeDtypeStruct((8, 5), F32),
                jax.ShapeDtypeStruct((8, 1024), F32),
            ),
            in_specs=[pl.BlockSpec(memory_space=pl.ANY)] * 6,
            out_specs=[pl.BlockSpec(memory_space=pltpu.VMEM)] * 2,
            scratch_shapes=[
                tiles,
                pltpu.VMEM((1, 8), jnp.int32),
                pltpu.VMEM((1, 64), jnp.int32),
                pltpu.VMEM((256, 256), BF16),
                pltpu.VMEM((256, 256), BF16),
                pltpu.VMEM((8, 40), BF16),
                pltpu.VMEM((5, 8, 8, 1024), BF16),
                *[tiles] * 7,
                *[pieces] * 5,
                pltpu.SemaphoreType.DMA((6,)),
                pltpu.SemaphoreType.DMA((4,)),
                pltpu.SemaphoreType.DMA((4,)),
                *[sems] * 16,
            ],
            compiler_params=pltpu.CompilerParams(
                collective_id=0, has_side_effects=True, vmem_limit_bytes=40 << 20
            ),
        )(three_center, tile_live, pair_atoms.reshape(1, 64), green_occ, green_vir, screened)

    placed = (P("aux", "pair", None), P("aux", "pair"), P(), P(), P(), P("aux", None))
    return jax.shard_map(
        per_device,
        mesh=mesh,
        in_specs=placed,
        out_specs=(P("aux", "pair"), P("pair", None)),
        check_vma=False,
    )
```

```python
import functools
import math

import jax
import jax.numpy as jnp
from jax import lax
from jax.experimental import pallas as pl
from jax.experimental.pallas import tpu as pltpu
from jax.sharding import PartitionSpec as P

MESH = pl.DeviceIdType.MESH
OA = 32
NAT = 8
REACH = 2
NX = 4
NZ = 16
F32 = jnp.float32
BF16 = jnp.bfloat16


def dot(a, b, dims=((1,), (0,))):
    return lax.dot_general(a, b, (dims, ((), ())), preferred_element_type=F32)


def iota(shape, dim):
    return lax.broadcasted_iota(jnp.int32, shape, dim)


def exchange_groups(parts):
    x0, x1, x2, x3 = parts
    lane = iota(x0.shape, 1)
    low = lane < 64
    even = (lane & 32) == 0
    y0 = jnp.where(low, x0, pltpu.roll(x2, 64, 1))
    y2 = jnp.where(low, pltpu.roll(x0, 64, 1), x2)
    y1 = jnp.where(low, x1, pltpu.roll(x3, 64, 1))
    y3 = jnp.where(low, pltpu.roll(x1, 64, 1), x3)
    z0 = jnp.where(even, y0, pltpu.roll(y1, 32, 1))
    z1 = jnp.where(even, pltpu.roll(y0, 96, 1), y1)
    z2 = jnp.where(even, y2, pltpu.roll(y3, 32, 1))
    z3 = jnp.where(even, pltpu.roll(y2, 96, 1), y3)
    return z0, z1, z2, z3


def to_matrix(tiles):
    cols = [tiles[:, g * 128 : (g + 1) * 128].reshape(2, 4, 8, 128) for g in range(8)]
    parts = [
        jnp.concatenate([c[:, bl] for c in cols], axis=0).reshape(128, 128) for bl in range(4)
    ]
    out = [z.reshape(8, 2, 8, 128) for z in exchange_groups(parts)]
    halves = [
        jnp.stack([z[:, bh] for z in out], axis=1).reshape(256, 128) for bh in range(2)
    ]
    return jnp.concatenate(halves, axis=1)


def to_tiles(matrix):
    halves = [matrix[:, bh * 128 : (bh + 1) * 128].reshape(8, 4, 8, 128) for bh in range(2)]
    parts = [
        jnp.stack([h[:, r] for h in halves], axis=1).reshape(128, 128) for r in range(4)
    ]
    out = [z.reshape(8, 2, 8, 128) for z in exchange_groups(parts)]
    cols = [
        jnp.stack([z[g] for z in out], axis=1).reshape(64, 128) for g in range(8)
    ]
    return jnp.concatenate(cols, axis=1)


def rows64(value):
    return value.astype(F32).reshape(64, value.shape[-1])


def kernel(
    n_aux,
    n_pair,
    tc_hbm,
    live_hbm,
    atoms_hbm,
    occ_hbm,
    vir_hbm,
    scr_hbm,
    pol_ref,
    self_ref,
    tc,
    live,
    atoms,
    occ,
    vir,
    scr,
    win,
    mt,
    zo,
    zt,
    vo,
    vt,
    xo,
    xr,
    chi,
    ar,
    fin,
    in_sem,
    s_win,
    r_win,
    s_m,
    r_m,
    s_z,
    r_z,
    s_v,
    r_v,
    s_x,
    r_x,
    s_c,
    r_c,
    s_a,
    r_a,
    s_f,
    r_f,
):
    a_me = lax.axis_index("aux")
    p_me = lax.axis_index("pair")
    x_me, z_me = a_me // NZ, a_me % NZ

    loads = [
        pltpu.make_async_copy(src, dst, in_sem.at[i])
        for i, (src, dst) in enumerate(
            (
                (tc_hbm, tc),
                (live_hbm, live),
                (atoms_hbm, atoms),
                (occ_hbm, occ),
                (vir_hbm, vir),
                (scr_hbm, scr),
            )
        )
    ]
    for c in loads:
        c.start()

    def by_pair(step):
        q = lax.rem(p_me + step, n_pair)
        return q, (a_me, q)

    def by_plane(step):
        q = lax.rem(p_me + step % 8, n_pair)
        x = lax.rem(x_me + step // 8, NX)
        return q, x, (x * NZ + z_me, q)

    def by_z(step):
        z = lax.rem(z_me + step, NZ)
        return z, (x_me * NZ + z, p_me)

    def by_x(step):
        x = lax.rem(x_me + step, NX)
        return x, (x * NZ + z_me, p_me)

    offsets = (1, -1, 2, -2)

    def by_window(d):
        return (lax.rem(a_me + d + n_aux, n_aux), p_me)

    barrier = pltpu.get_barrier_semaphore()
    peers = [by_z(step)[-1] for step in range(1, NZ)]
    peers += [by_plane(step)[-1] for step in range(1, 32)]
    peers += [by_window(d) for d in offsets]
    for device in peers:
        pl.semaphore_signal(barrier, inc=1, device_id=device, device_id_type=MESH)

    def remote(src, dst, send, recv, device):
        return pltpu.make_async_remote_copy(
            src_ref=src,
            dst_ref=dst,
            send_sem=send,
            recv_sem=recv,
            device_id=device,
            device_id_type=MESH,
        )

    def exchange(peer, count, source, dest, send, recv):
        copies = []
        for step in range(1, count):
            *there, device = peer(step)
            copies.append(remote(source(*there), dest, send.at[step - 1], recv.at[step - 1], device))
        for c in copies:
            c.start()
        return copies

    loads[0].wait()
    loads[1].wait()
    eye8 = iota((8, 8), 0) == iota((8, 8), 1)
    live_col = jnp.sum(
        jnp.where(eye8, jnp.broadcast_to(live[...].astype(F32), (8, 8)), 0.0), axis=1, keepdims=True
    )
    win[REACH] = (tc[...].astype(F32) * live_col[None]).astype(BF16)

    pl.semaphore_wait(barrier, len(peers))
    started = []
    window_copies = {}
    for i, d in enumerate(offsets):
        c = remote(win.at[REACH], win.at[REACH - d], s_win.at[i], r_win.at[i], by_window(d))
        c.start()
        window_copies[REACH - d] = c
        started.append(c)
    m_copies = exchange(by_pair, 8, lambda q: win.at[REACH, q], mt.at[p_me], s_m, r_m)
    started += m_copies
    mt[p_me] = win[REACH, p_me]

    for c in loads[2:]:
        c.wait()
    new = iota((256, 256), 0)
    old = iota((256, 256), 1)
    perm = jnp.where((new % 8) * 32 + new // 8 == old, 1.0, 0.0).astype(BF16)
    occ_cols = dot(occ[...], perm, ((1,), (1,))).astype(BF16)
    occ_both = dot(perm, occ_cols).astype(BF16)
    atom_row = atoms[...]
    place = iota((64, 64), 0)
    pick = jnp.where((place % 8) * 8 + place // 8 == atom_row, 1.0, 0.0).astype(BF16)
    eye64 = iota((64, 64), 0) == iota((64, 64), 1)
    atom_col = jnp.sum(
        jnp.where(eye64, jnp.broadcast_to(atom_row.astype(F32), (64, 64)), 0.0), axis=1, keepdims=True
    ).astype(jnp.int32)
    spot = iota((64, 64), 1)
    put = jnp.where((spot % 8) * 8 + spot // 8 == atom_col, 1.0, 0.0).astype(BF16)
    wide = jnp.broadcast_to(scr[...].astype(F32)[:, None, :], (8, 8, 40)).reshape(64, 40).astype(BF16)
    same_tile = (iota((64, 64), 0) % 8) == (iota((64, 64), 1) % 8)
    couple = []
    for slot in range(5):
        spread = jnp.where(iota((40, 64), 0) == slot * 8 + iota((40, 64), 1) // 8, 1.0, 0.0)
        block = a_me + slot - REACH
        inside = jnp.logical_and(block >= 0, block < n_aux)
        keep = jnp.logical_and(same_tile, inside)
        couple.append(jnp.where(keep, dot(wide, spread.astype(BF16)), 0.0).astype(BF16))

    for c in m_copies:
        c.wait_recv()
    form = to_matrix(dot(pick, rows64(mt[...]).astype(BF16))).astype(BF16)
    left = dot(occ_both, form, ((0,), (0,))).astype(BF16)
    product = dot(left, vir[...])
    z_tiles = dot(put, to_tiles(product).astype(BF16))
    zo[...] = z_tiles.reshape(8, 8, 1024).astype(BF16)
    z_copies = exchange(by_pair, 8, lambda q: zo.at[q], zt.at[p_me], s_z, r_z)
    started += z_copies
    zt[p_me] = zo[p_me]

    mixed = dot(couple[2], rows64(win[2]).astype(BF16))
    for slot in (1, 3, 0, 4):
        window_copies[slot].wait_recv()
        mixed += dot(couple[slot], rows64(win[slot]).astype(BF16))
    vo[...] = mixed.reshape(8, 8, 1024).astype(BF16)
    v_copies = exchange(by_pair, 8, lambda q: vo.at[q], vt.at[p_me], s_v, r_v)
    started += v_copies
    vt[p_me] = vo[p_me]

    for c in z_copies:
        c.wait_recv()
    z_rows = rows64(zt[...]).astype(BF16)
    chi_total = jnp.zeros((8, 128), F32)
    for slot in range(5):
        terms = dot(z_rows, rows64(win[slot]).astype(BF16), ((1,), (1,)))
        block = a_me + slot - REACH
        inside = jnp.logical_and(block >= 0, block < n_aux)
        keep = jnp.logical_and(same_tile, inside)
        terms = jnp.sum(jnp.where(keep, terms, 0.0).reshape(8, 8, 64), axis=1)
        gather = jnp.where(iota((64, 128), 1) == slot * 8 + iota((64, 128), 0) // 8, 1.0, 0.0)
        chi_total += jnp.dot(terms, gather, precision=lax.Precision.HIGHEST, preferred_element_type=F32)
    chi[p_me] = chi_total * (1.0 / (OA * NAT))
    c_copies = exchange(by_pair, 8, lambda q: chi.at[p_me], chi.at[p_me], s_c, r_c)
    started += c_copies

    for c in v_copies:
        c.wait_recv()
    v_form = to_matrix(dot(pick, rows64(vt[...]).astype(BF16))).astype(BF16)
    scaled = dot(v_form, occ_cols).astype(BF16)
    energy = dot(scaled, form)
    energy_tiles = dot(put, to_tiles(energy).astype(BF16))
    for x in range(NX):
        xo[:, x] = energy_tiles[:, x * 256 : (x + 1) * 256].reshape(8, 8, 256).astype(BF16)
    x_copies = exchange(by_plane, 32, lambda q, x: xo.at[q, x], xr.at[x_me * 8 + p_me], s_x, r_x)
    xr[x_me * 8 + p_me] = xo[p_me, x_me]

    for c in c_copies:
        c.wait_recv()
    chi_sum = jnp.sum(chi[...], axis=0)
    turned = pltpu.roll(chi_sum, lax.rem(128 - 5 * p_me, 128), 1)
    pol_ref[...] = turned[:, :5]

    for c in x_copies:
        c.wait_recv()
    ar[z_me] = jnp.sum(xr[...].astype(F32), axis=0).astype(BF16)
    a_copies = exchange(by_z, NZ, lambda z: ar.at[z_me], ar.at[z_me], s_a, r_a)
    for c in started + x_copies:
        c.wait_send()
    for c in a_copies:
        c.wait_recv()
    scale = -1.0 / math.sqrt(n_aux * 8 * NAT * OA * NAT)
    fin[x_me] = jnp.sum(ar[...].astype(F32), axis=0) * scale
    f_copies = exchange(by_x, NX, lambda x: fin.at[x_me], fin.at[x_me], s_f, r_f)
    for c in a_copies:
        c.wait_send()
    for c in f_copies:
        c.wait_recv()
    for x in range(NX):
        self_ref[:, x * 256 : (x + 1) * 256] = fin[x]
    for c in f_copies:
        c.wait_send()


def solution(mesh):
    n_aux, n_pair = mesh.shape["aux"], mesh.shape["pair"]

    def per_device(three_center, tile_live, pair_atoms, green_occ, green_vir, screened):
        tiles = pltpu.VMEM((8, 8, 1024), BF16)
        sems = pltpu.SemaphoreType.DMA((7,))
        return pl.pallas_call(
            functools.partial(kernel, n_aux, n_pair),
            out_shape=(
                jax.ShapeDtypeStruct((8, 5), F32),
                jax.ShapeDtypeStruct((8, 1024), F32),
            ),
            in_specs=[pl.BlockSpec(memory_space=pl.ANY)] * 6,
            out_specs=[pl.BlockSpec(memory_space=pltpu.VMEM)] * 2,
            scratch_shapes=[
                tiles,
                pltpu.VMEM((1, 8), jnp.int32),
                pltpu.VMEM((1, 64), jnp.int32),
                pltpu.VMEM((256, 256), BF16),
                pltpu.VMEM((256, 256), BF16),
                pltpu.VMEM((8, 40), BF16),
                pltpu.VMEM((5, 8, 8, 1024), BF16),
                *[tiles] * 5,
                pltpu.VMEM((8, NX, 8, 256), BF16),
                pltpu.VMEM((32, 8, 256), BF16),
                pltpu.VMEM((8, 8, 128), F32),
                pltpu.VMEM((NZ, 8, 256), BF16),
                pltpu.VMEM((NX, 8, 256), F32),
                pltpu.SemaphoreType.DMA((6,)),
                pltpu.SemaphoreType.DMA((4,)),
                pltpu.SemaphoreType.DMA((4,)),
                *[sems] * 6,
                *[pltpu.SemaphoreType.DMA((31,))] * 2,
                *[sems] * 2,
                *[pltpu.SemaphoreType.DMA((15,))] * 2,
                *[sems] * 2,
            ],
            compiler_params=pltpu.CompilerParams(
                collective_id=0, has_side_effects=True, vmem_limit_bytes=40 << 20
            ),
        )(
            *(
                pltpu.with_memory_space_constraint(v, pltpu.HBM)
                for v in (
                    three_center,
                    tile_live,
                    pair_atoms.reshape(1, 64),
                    green_occ,
                    green_vir,
                    screened,
                )
            )
        )

    placed = (P("aux", "pair", None), P("aux", "pair"), P(), P(), P(), P("aux", None))
    return jax.shard_map(
        per_device,
        mesh=mesh,
        in_specs=placed,
        out_specs=(P("aux", "pair"), P("pair", None)),
        check_vma=False,
    )
```

```python
import functools
import math

import jax
import jax.numpy as jnp
from jax import lax
from jax.experimental import pallas as pl
from jax.experimental.pallas import tpu as pltpu
from jax.sharding import PartitionSpec as P

MESH = pl.DeviceIdType.MESH
OA = 32
NAT = 8
REACH = 2
NX = 4
NZ = 16
F32 = jnp.float32
BF16 = jnp.bfloat16


def dot(a, b, dims=((1,), (0,))):
    return lax.dot_general(a, b, (dims, ((), ())), preferred_element_type=F32)


def iota(shape, dim):
    return lax.broadcasted_iota(jnp.int32, shape, dim)


def exchange_groups(parts):
    x0, x1, x2, x3 = parts
    lane = iota(x0.shape, 1)
    low = lane < 64
    even = (lane & 32) == 0
    y0 = jnp.where(low, x0, pltpu.roll(x2, 64, 1))
    y2 = jnp.where(low, pltpu.roll(x0, 64, 1), x2)
    y1 = jnp.where(low, x1, pltpu.roll(x3, 64, 1))
    y3 = jnp.where(low, pltpu.roll(x1, 64, 1), x3)
    z0 = jnp.where(even, y0, pltpu.roll(y1, 32, 1))
    z1 = jnp.where(even, pltpu.roll(y0, 96, 1), y1)
    z2 = jnp.where(even, y2, pltpu.roll(y3, 32, 1))
    z3 = jnp.where(even, pltpu.roll(y2, 96, 1), y3)
    return z0, z1, z2, z3


def to_matrix(tiles):
    cols = [tiles[:, g * 128 : (g + 1) * 128].reshape(2, 4, 8, 128) for g in range(8)]
    parts = [
        jnp.concatenate([c[:, bl] for c in cols], axis=0).reshape(128, 128) for bl in range(4)
    ]
    out = [z.reshape(8, 2, 8, 128) for z in exchange_groups(parts)]
    halves = [
        jnp.stack([z[:, bh] for z in out], axis=1).reshape(256, 128) for bh in range(2)
    ]
    return jnp.concatenate(halves, axis=1)


def to_tiles(matrix):
    halves = [matrix[:, bh * 128 : (bh + 1) * 128].reshape(8, 4, 8, 128) for bh in range(2)]
    parts = [
        jnp.stack([h[:, r] for h in halves], axis=1).reshape(128, 128) for r in range(4)
    ]
    out = [z.reshape(8, 2, 8, 128) for z in exchange_groups(parts)]
    cols = [
        jnp.stack([z[g] for z in out], axis=1).reshape(64, 128) for g in range(8)
    ]
    return jnp.concatenate(cols, axis=1)


def rows64(value):
    return value.astype(F32).reshape(64, value.shape[-1])


def kernel(
    n_aux,
    n_pair,
    tc_hbm,
    live_hbm,
    atoms_hbm,
    occ_hbm,
    vir_hbm,
    scr_hbm,
    pol_ref,
    self_ref,
    tc,
    live,
    atoms,
    occ,
    vir,
    scr,
    win,
    mt,
    zo,
    zt,
    vo,
    vt,
    xo,
    xr,
    chi,
    ar,
    fin,
    in_sem,
    s_win,
    r_win,
    s_m,
    r_m,
    s_z,
    r_z,
    s_v,
    r_v,
    s_x,
    r_x,
    s_c,
    r_c,
    s_a,
    r_a,
    s_f,
    r_f,
    known,
):
    a_me = lax.axis_index("aux")
    p_me = lax.axis_index("pair")
    x_me, z_me = a_me // NZ, a_me % NZ

    loads = [
        pltpu.make_async_copy(src, dst, in_sem.at[i])
        for i, (src, dst) in enumerate(
            (
                (tc_hbm, tc),
                (live_hbm, live),
                (atoms_hbm, atoms),
                (occ_hbm, occ),
                (vir_hbm, vir),
                (scr_hbm, scr),
            )
        )
    ]
    for c in loads:
        c.start()

    def by_pair(step):
        q = lax.rem(p_me + step, n_pair)
        return q, (a_me, q)

    def by_plane(step):
        q = lax.rem(p_me + step % 8, n_pair)
        x = lax.rem(x_me + step // 8, NX)
        return q, x, (x * NZ + z_me, q)

    def by_z(step):
        z = lax.rem(z_me + step, NZ)
        return z, (x_me * NZ + z, p_me)

    def by_x(step):
        x = lax.rem(x_me + step, NX)
        return x, (x * NZ + z_me, p_me)

    offsets = (1, -1, 2, -2)

    def by_window(d):
        return (lax.rem(a_me + d + n_aux, n_aux), p_me)

    barrier = pltpu.get_barrier_semaphore()
    near = (1, NZ - 1, 2, NZ - 2)
    peers = [by_window(d) for d in offsets]
    peers += [by_x(step)[-1] for step in (2, 1, 3)]
    peers += [by_pair(step)[-1] for step in range(1, 8)]
    peers += [by_z(step)[-1] for step in near]
    for device in peers:
        pl.semaphore_signal(barrier, inc=1, device_id=device, device_id_type=MESH)

    def remote(src, dst, send, recv, device):
        return pltpu.make_async_remote_copy(
            src_ref=src,
            dst_ref=dst,
            send_sem=send,
            recv_sem=recv,
            device_id=device,
            device_id_type=MESH,
        )

    def exchange(peer, count, source, dest, send, recv):
        copies = []
        for step in range(1, count):
            *there, device = peer(step)
            copies.append(remote(source(*there), dest, send.at[step - 1], recv.at[step - 1], device))
        for c in copies:
            c.start()
        return copies

    loads[0].wait()
    loads[1].wait()
    eye8 = iota((8, 8), 0) == iota((8, 8), 1)
    live_col = jnp.sum(
        jnp.where(eye8, jnp.broadcast_to(live[...].astype(F32), (8, 8)), 0.0), axis=1, keepdims=True
    )
    win[REACH] = (tc[...].astype(F32) * live_col[None]).astype(BF16)

    pl.semaphore_wait(barrier, len(peers))
    for step in (2, NZ - 2):
        pl.semaphore_signal(known.at[0], inc=1, device_id=by_z(step)[-1], device_id_type=MESH)
    started = []
    window_copies = {}
    for i, d in enumerate(offsets):
        c = remote(win.at[REACH], win.at[REACH - d], s_win.at[i], r_win.at[i], by_window(d))
        c.start()
        window_copies[REACH - d] = c
        started.append(c)
    m_copies = exchange(by_pair, 8, lambda q: win.at[REACH, q], mt.at[p_me], s_m, r_m)
    started += m_copies
    mt[p_me] = win[REACH, p_me]

    for c in loads[2:]:
        c.wait()
    new = iota((256, 256), 0)
    old = iota((256, 256), 1)
    perm = jnp.where((new % 8) * 32 + new // 8 == old, 1.0, 0.0).astype(BF16)
    occ_cols = dot(occ[...], perm, ((1,), (1,))).astype(BF16)
    occ_both = dot(perm, occ_cols).astype(BF16)
    atom_row = atoms[...]
    place = iota((64, 64), 0)
    pick = jnp.where((place % 8) * 8 + place // 8 == atom_row, 1.0, 0.0).astype(BF16)
    eye64 = iota((64, 64), 0) == iota((64, 64), 1)
    atom_col = jnp.sum(
        jnp.where(eye64, jnp.broadcast_to(atom_row.astype(F32), (64, 64)), 0.0), axis=1, keepdims=True
    ).astype(jnp.int32)
    spot = iota((64, 64), 1)
    put = jnp.where((spot % 8) * 8 + spot // 8 == atom_col, 1.0, 0.0).astype(BF16)
    wide = jnp.broadcast_to(scr[...].astype(F32)[:, None, :], (8, 8, 40)).reshape(64, 40).astype(BF16)
    same_tile = (iota((64, 64), 0) % 8) == (iota((64, 64), 1) % 8)
    couple = []
    for slot in range(5):
        spread = jnp.where(iota((40, 64), 0) == slot * 8 + iota((40, 64), 1) // 8, 1.0, 0.0)
        block = a_me + slot - REACH
        inside = jnp.logical_and(block >= 0, block < n_aux)
        keep = jnp.logical_and(same_tile, inside)
        couple.append(jnp.where(keep, dot(wide, spread.astype(BF16)), 0.0).astype(BF16))

    for c in m_copies:
        c.wait_recv()
    form = to_matrix(dot(pick, rows64(mt[...]).astype(BF16))).astype(BF16)
    left = dot(occ_both, form, ((0,), (0,))).astype(BF16)
    product = dot(left, vir[...])
    z_tiles = dot(put, to_tiles(product).astype(BF16))
    zo[...] = z_tiles.reshape(8, 8, 1024).astype(BF16)
    z_copies = exchange(by_pair, 8, lambda q: zo.at[q], zt.at[p_me], s_z, r_z)
    started += z_copies
    zt[p_me] = zo[p_me]

    pl.semaphore_wait(known.at[0], 2)
    for step in (4, NZ - 4):
        pl.semaphore_signal(known.at[1], inc=1, device_id=by_z(step)[-1], device_id_type=MESH)

    mixed = dot(couple[2], rows64(win[2]).astype(BF16))
    for slot in (1, 3, 0, 4):
        window_copies[slot].wait_recv()
        mixed += dot(couple[slot], rows64(win[slot]).astype(BF16))
    vo[...] = mixed.reshape(8, 8, 1024).astype(BF16)
    v_copies = exchange(by_pair, 8, lambda q: vo.at[q], vt.at[p_me], s_v, r_v)
    started += v_copies
    vt[p_me] = vo[p_me]

    for c in z_copies:
        c.wait_recv()
    z_rows = rows64(zt[...]).astype(BF16)
    chi_total = jnp.zeros((8, 128), F32)
    for slot in range(5):
        terms = dot(z_rows, rows64(win[slot]).astype(BF16), ((1,), (1,)))
        block = a_me + slot - REACH
        inside = jnp.logical_and(block >= 0, block < n_aux)
        keep = jnp.logical_and(same_tile, inside)
        terms = jnp.sum(jnp.where(keep, terms, 0.0).reshape(8, 8, 64), axis=1)
        gather = jnp.where(iota((64, 128), 1) == slot * 8 + iota((64, 128), 0) // 8, 1.0, 0.0)
        chi_total += jnp.dot(terms, gather, precision=lax.Precision.HIGHEST, preferred_element_type=F32)
    chi[p_me] = chi_total * (1.0 / (OA * NAT))
    c_copies = exchange(by_pair, 8, lambda q: chi.at[p_me], chi.at[p_me], s_c, r_c)
    started += c_copies

    for c in v_copies:
        c.wait_recv()
    v_form = to_matrix(dot(pick, rows64(vt[...]).astype(BF16))).astype(BF16)
    scaled = dot(v_form, occ_cols).astype(BF16)
    energy = dot(scaled, form)
    energy_tiles = dot(put, to_tiles(energy).astype(BF16))
    for x in range(NX):
        xo[:, x] = energy_tiles[:, x * 256 : (x + 1) * 256].reshape(8, 8, 256).astype(BF16)
    x_copies = exchange(by_plane, 32, lambda q, x: xo.at[q, x], xr.at[x_me * 8 + p_me], s_x, r_x)
    xr[x_me * 8 + p_me] = xo[p_me, x_me]

    for c in c_copies:
        c.wait_recv()
    chi_sum = jnp.sum(chi[...], axis=0)
    turned = pltpu.roll(chi_sum, lax.rem(128 - 5 * p_me, 128), 1)
    pol_ref[...] = turned[:, :5]

    for c in x_copies:
        c.wait_recv()
    ar[z_me] = jnp.sum(xr[...].astype(F32), axis=0).astype(BF16)
    pl.semaphore_wait(known.at[1], 2)
    a_copies = exchange(by_z, NZ, lambda z: ar.at[z_me], ar.at[z_me], s_a, r_a)
    for c in started + x_copies:
        c.wait_send()
    for c in a_copies:
        c.wait_recv()
    scale = -1.0 / math.sqrt(n_aux * 8 * NAT * OA * NAT)
    fin[x_me] = jnp.sum(ar[...].astype(F32), axis=0) * scale
    f_copies = exchange(by_x, NX, lambda x: fin.at[x_me], fin.at[x_me], s_f, r_f)
    for c in a_copies:
        c.wait_send()
    for c in f_copies:
        c.wait_recv()
    for x in range(NX):
        self_ref[:, x * 256 : (x + 1) * 256] = fin[x]
    for c in f_copies:
        c.wait_send()


def solution(mesh):
    n_aux, n_pair = mesh.shape["aux"], mesh.shape["pair"]

    def per_device(three_center, tile_live, pair_atoms, green_occ, green_vir, screened):
        tiles = pltpu.VMEM((8, 8, 1024), BF16)
        sems = pltpu.SemaphoreType.DMA((7,))
        return pl.pallas_call(
            functools.partial(kernel, n_aux, n_pair),
            out_shape=(
                jax.ShapeDtypeStruct((8, 5), F32),
                jax.ShapeDtypeStruct((8, 1024), F32),
            ),
            in_specs=[pl.BlockSpec(memory_space=pl.ANY)] * 6,
            out_specs=[pl.BlockSpec(memory_space=pltpu.VMEM)] * 2,
            scratch_shapes=[
                tiles,
                pltpu.VMEM((1, 8), jnp.int32),
                pltpu.VMEM((1, 64), jnp.int32),
                pltpu.VMEM((256, 256), BF16),
                pltpu.VMEM((256, 256), BF16),
                pltpu.VMEM((8, 40), BF16),
                pltpu.VMEM((5, 8, 8, 1024), BF16),
                *[tiles] * 5,
                pltpu.VMEM((8, NX, 8, 256), BF16),
                pltpu.VMEM((32, 8, 256), BF16),
                pltpu.VMEM((8, 8, 128), F32),
                pltpu.VMEM((NZ, 8, 256), BF16),
                pltpu.VMEM((NX, 8, 256), F32),
                pltpu.SemaphoreType.DMA((6,)),
                pltpu.SemaphoreType.DMA((4,)),
                pltpu.SemaphoreType.DMA((4,)),
                *[sems] * 6,
                *[pltpu.SemaphoreType.DMA((31,))] * 2,
                *[sems] * 2,
                *[pltpu.SemaphoreType.DMA((15,))] * 2,
                *[sems] * 2,
                pltpu.SemaphoreType.REGULAR((2,)),
            ],
            compiler_params=pltpu.CompilerParams(
                collective_id=0, has_side_effects=True, vmem_limit_bytes=40 << 20
            ),
        )(
            *(
                pltpu.with_memory_space_constraint(v, pltpu.HBM)
                for v in (
                    three_center,
                    tile_live,
                    pair_atoms.reshape(1, 64),
                    green_occ,
                    green_vir,
                    screened,
                )
            )
        )

    placed = (P("aux", "pair", None), P("aux", "pair"), P(), P(), P(), P("aux", None))
    return jax.shard_map(
        per_device,
        mesh=mesh,
        in_specs=placed,
        out_specs=(P("aux", "pair"), P("pair", None)),
        check_vma=False,
    )
```

```python
import functools
import math

import jax
import jax.numpy as jnp
from jax import lax
from jax.experimental import pallas as pl
from jax.experimental.pallas import tpu as pltpu
from jax.sharding import PartitionSpec as P

MESH = pl.DeviceIdType.MESH
OA = 32
NAT = 8
REACH = 2
NX = 4
NZ = 16
F32 = jnp.float32
BF16 = jnp.bfloat16


def dot(a, b, dims=((1,), (0,))):
    return lax.dot_general(a, b, (dims, ((), ())), preferred_element_type=F32)


def iota(shape, dim):
    return lax.broadcasted_iota(jnp.int32, shape, dim)


def exchange_groups(parts):
    x0, x1, x2, x3 = parts
    lane = iota(x0.shape, 1)
    low = lane < 64
    even = (lane & 32) == 0
    y0 = jnp.where(low, x0, pltpu.roll(x2, 64, 1))
    y2 = jnp.where(low, pltpu.roll(x0, 64, 1), x2)
    y1 = jnp.where(low, x1, pltpu.roll(x3, 64, 1))
    y3 = jnp.where(low, pltpu.roll(x1, 64, 1), x3)
    z0 = jnp.where(even, y0, pltpu.roll(y1, 32, 1))
    z1 = jnp.where(even, pltpu.roll(y0, 96, 1), y1)
    z2 = jnp.where(even, y2, pltpu.roll(y3, 32, 1))
    z3 = jnp.where(even, pltpu.roll(y2, 96, 1), y3)
    return z0, z1, z2, z3


def to_matrix(tiles):
    cols = [tiles[:, g * 128 : (g + 1) * 128].reshape(2, 4, 8, 128) for g in range(8)]
    parts = [
        jnp.concatenate([c[:, bl] for c in cols], axis=0).reshape(128, 128) for bl in range(4)
    ]
    out = [z.reshape(8, 2, 8, 128) for z in exchange_groups(parts)]
    halves = [
        jnp.stack([z[:, bh] for z in out], axis=1).reshape(256, 128) for bh in range(2)
    ]
    return jnp.concatenate(halves, axis=1)


def to_tiles(matrix):
    halves = [matrix[:, bh * 128 : (bh + 1) * 128].reshape(8, 4, 8, 128) for bh in range(2)]
    parts = [
        jnp.stack([h[:, r] for h in halves], axis=1).reshape(128, 128) for r in range(4)
    ]
    out = [z.reshape(8, 2, 8, 128) for z in exchange_groups(parts)]
    cols = [
        jnp.stack([z[g] for z in out], axis=1).reshape(64, 128) for g in range(8)
    ]
    return jnp.concatenate(cols, axis=1)


def rows64(value):
    return value.astype(F32).reshape(64, value.shape[-1])


def kernel(
    n_aux,
    n_pair,
    tc_hbm,
    live_hbm,
    atoms_hbm,
    occ_hbm,
    vir_hbm,
    scr_hbm,
    pol_ref,
    self_ref,
    tc,
    live,
    atoms,
    occ,
    vir,
    scr,
    win,
    mt,
    zo,
    zt,
    vo,
    vt,
    xo,
    xr,
    chi,
    ar,
    fin,
    in_sem,
    s_win,
    r_win,
    s_far,
    r_far,
    s_m,
    r_m,
    s_z,
    r_z,
    s_v,
    r_v,
    s_x,
    r_x,
    s_c,
    r_c,
    s_a,
    r_a,
    s_f,
    r_f,
    known,
):
    a_me = lax.axis_index("aux")
    p_me = lax.axis_index("pair")
    x_me, z_me = a_me // NZ, a_me % NZ

    loads = [
        pltpu.make_async_copy(src, dst, in_sem.at[i])
        for i, (src, dst) in enumerate(
            (
                (tc_hbm, tc),
                (live_hbm, live),
                (atoms_hbm, atoms),
                (occ_hbm, occ),
                (vir_hbm, vir),
                (scr_hbm, scr),
            )
        )
    ]
    for c in loads:
        c.start()

    def by_pair(step):
        q = lax.rem(p_me + step, n_pair)
        return q, (a_me, q)

    def by_plane(step):
        q = lax.rem(p_me + step % 8, n_pair)
        x = lax.rem(x_me + step // 8, NX)
        return q, x, (x * NZ + z_me, q)

    def by_z(step):
        z = lax.rem(z_me + step, NZ)
        return z, (x_me * NZ + z, p_me)

    def by_x(step):
        x = lax.rem(x_me + step, NX)
        return x, (x * NZ + z_me, p_me)

    offsets = (1, -1)
    chunks = [pl.ds(2 * c, 2) for c in range(4)]

    def by_window(d):
        return (lax.rem(a_me + d + n_aux, n_aux), p_me)

    barrier = pltpu.get_barrier_semaphore()
    peers = [by_window(d) for d in offsets]
    peers += [by_x(step)[-1] for step in (2, 1, 3)]
    peers += [by_pair(step)[-1] for step in range(1, 8)]
    peers += [by_z(step)[-1] for step in (1, NZ - 1)]
    for device in peers:
        pl.semaphore_signal(barrier, inc=1, device_id=device, device_id_type=MESH)

    def tell(r):
        for step in (1 << r, NZ - (1 << r)):
            pl.semaphore_signal(known.at[r], inc=1, device_id=by_z(step)[-1], device_id_type=MESH)

    def hear(r):
        pl.semaphore_wait(known.at[r], 2)

    def remote(src, dst, send, recv, device):
        return pltpu.make_async_remote_copy(
            src_ref=src,
            dst_ref=dst,
            send_sem=send,
            recv_sem=recv,
            device_id=device,
            device_id_type=MESH,
        )

    def exchange(peer, count, source, dest, send, recv):
        copies = []
        for step in range(1, count):
            *there, device = peer(step)
            copies.append(remote(source(*there), dest, send.at[step - 1], recv.at[step - 1], device))
        for c in copies:
            c.start()
        return copies

    loads[0].wait()
    loads[1].wait()
    eye8 = iota((8, 8), 0) == iota((8, 8), 1)
    live_col = jnp.sum(
        jnp.where(eye8, jnp.broadcast_to(live[...].astype(F32), (8, 8)), 0.0), axis=1, keepdims=True
    )
    win[REACH] = (tc[...].astype(F32) * live_col[None]).astype(BF16)

    pl.semaphore_wait(barrier, len(peers))
    started = []
    arriving = {1: [], 3: []}
    for c, part in enumerate(chunks):
        for i, d in enumerate(offsets):
            copy = remote(
                win.at[REACH, part], win.at[REACH - d, part], s_win.at[i, c], r_win.at[i, c], by_window(d)
            )
            copy.start()
            arriving[REACH - d].append(copy)
    m_copies = exchange(by_pair, 8, lambda q: win.at[REACH, q], mt.at[p_me], s_m, r_m)
    started += m_copies
    mt[p_me] = win[REACH, p_me]

    for c in loads[2:]:
        c.wait()
    new = iota((256, 256), 0)
    old = iota((256, 256), 1)
    perm = jnp.where((new % 8) * 32 + new // 8 == old, 1.0, 0.0).astype(BF16)
    occ_cols = dot(occ[...], perm, ((1,), (1,))).astype(BF16)
    occ_both = dot(perm, occ_cols).astype(BF16)
    atom_row = atoms[...]
    place = iota((64, 64), 0)
    pick = jnp.where((place % 8) * 8 + place // 8 == atom_row, 1.0, 0.0).astype(BF16)
    eye64 = iota((64, 64), 0) == iota((64, 64), 1)
    atom_col = jnp.sum(
        jnp.where(eye64, jnp.broadcast_to(atom_row.astype(F32), (64, 64)), 0.0), axis=1, keepdims=True
    ).astype(jnp.int32)
    spot = iota((64, 64), 1)
    put = jnp.where((spot % 8) * 8 + spot // 8 == atom_col, 1.0, 0.0).astype(BF16)
    wide = jnp.broadcast_to(scr[...].astype(F32)[:, None, :], (8, 8, 40)).reshape(64, 40).astype(BF16)
    same_tile = (iota((64, 64), 0) % 8) == (iota((64, 64), 1) % 8)
    couple = []
    for slot in range(5):
        spread = jnp.where(iota((40, 64), 0) == slot * 8 + iota((40, 64), 1) // 8, 1.0, 0.0)
        block = a_me + slot - REACH
        inside = jnp.logical_and(block >= 0, block < n_aux)
        keep = jnp.logical_and(same_tile, inside)
        couple.append(jnp.where(keep, dot(wide, spread.astype(BF16)), 0.0).astype(BF16))

    tell(0)
    relayed = {0: [], 4: []}
    for c, part in enumerate(chunks):
        for i, d in enumerate(offsets):
            arriving[REACH - d][c].wait_recv()
            copy = remote(
                win.at[REACH - d, part],
                win.at[REACH - 2 * d, part],
                s_far.at[i, c],
                r_far.at[i, c],
                by_window(d),
            )
            copy.start()
            relayed[REACH - 2 * d].append(copy)
    started += arriving[1] + arriving[3] + relayed[0] + relayed[4]

    for c in m_copies:
        c.wait_recv()
    form = to_matrix(dot(pick, rows64(mt[...]).astype(BF16))).astype(BF16)
    left = dot(occ_both, form, ((0,), (0,))).astype(BF16)
    product = dot(left, vir[...])
    z_tiles = dot(put, to_tiles(product).astype(BF16))
    zo[...] = z_tiles.reshape(8, 8, 1024).astype(BF16)
    z_copies = exchange(by_pair, 8, lambda q: zo.at[q], zt.at[p_me], s_z, r_z)
    started += z_copies
    zt[p_me] = zo[p_me]

    hear(0)
    tell(1)
    mixed = dot(couple[2], rows64(win[2]).astype(BF16))
    for slot in (1, 3, 0, 4):
        for c in relayed.get(slot, ()):
            c.wait_recv()
        mixed += dot(couple[slot], rows64(win[slot]).astype(BF16))
    vo[...] = mixed.reshape(8, 8, 1024).astype(BF16)
    v_copies = exchange(by_pair, 8, lambda q: vo.at[q], vt.at[p_me], s_v, r_v)
    started += v_copies
    vt[p_me] = vo[p_me]

    hear(1)
    tell(2)
    for c in z_copies:
        c.wait_recv()
    z_rows = rows64(zt[...]).astype(BF16)
    chi_total = jnp.zeros((8, 128), F32)
    for slot in range(5):
        terms = dot(z_rows, rows64(win[slot]).astype(BF16), ((1,), (1,)))
        block = a_me + slot - REACH
        inside = jnp.logical_and(block >= 0, block < n_aux)
        keep = jnp.logical_and(same_tile, inside)
        terms = jnp.sum(jnp.where(keep, terms, 0.0).reshape(8, 8, 64), axis=1)
        gather = jnp.where(iota((64, 128), 1) == slot * 8 + iota((64, 128), 0) // 8, 1.0, 0.0)
        chi_total += jnp.dot(terms, gather, precision=lax.Precision.HIGHEST, preferred_element_type=F32)
    chi[p_me] = chi_total * (1.0 / (OA * NAT))
    c_copies = exchange(by_pair, 8, lambda q: chi.at[p_me], chi.at[p_me], s_c, r_c)
    started += c_copies

    for c in v_copies:
        c.wait_recv()
    v_form = to_matrix(dot(pick, rows64(vt[...]).astype(BF16))).astype(BF16)
    scaled = dot(v_form, occ_cols).astype(BF16)
    energy = dot(scaled, form)
    energy_tiles = dot(put, to_tiles(energy).astype(BF16))
    for x in range(NX):
        xo[:, x] = energy_tiles[:, x * 256 : (x + 1) * 256].reshape(8, 8, 256).astype(BF16)
    x_copies = exchange(by_plane, 32, lambda q, x: xo.at[q, x], xr.at[x_me * 8 + p_me], s_x, r_x)
    xr[x_me * 8 + p_me] = xo[p_me, x_me]

    for c in c_copies:
        c.wait_recv()
    chi_sum = jnp.sum(chi[...], axis=0)
    turned = pltpu.roll(chi_sum, lax.rem(128 - 5 * p_me, 128), 1)
    pol_ref[...] = turned[:, :5]

    for c in x_copies:
        c.wait_recv()
    ar[z_me] = jnp.sum(xr[...].astype(F32), axis=0).astype(BF16)
    hear(2)
    a_copies = exchange(by_z, NZ, lambda z: ar.at[z_me], ar.at[z_me], s_a, r_a)
    for c in started + x_copies:
        c.wait_send()
    for c in a_copies:
        c.wait_recv()
    scale = -1.0 / math.sqrt(n_aux * 8 * NAT * OA * NAT)
    fin[x_me] = jnp.sum(ar[...].astype(F32), axis=0) * scale
    f_copies = exchange(by_x, NX, lambda x: fin.at[x_me], fin.at[x_me], s_f, r_f)
    for c in a_copies:
        c.wait_send()
    for c in f_copies:
        c.wait_recv()
    for x in range(NX):
        self_ref[:, x * 256 : (x + 1) * 256] = fin[x]
    for c in f_copies:
        c.wait_send()


def solution(mesh):
    n_aux, n_pair = mesh.shape["aux"], mesh.shape["pair"]

    def per_device(three_center, tile_live, pair_atoms, green_occ, green_vir, screened):
        tiles = pltpu.VMEM((8, 8, 1024), BF16)
        sems = pltpu.SemaphoreType.DMA((7,))
        return pl.pallas_call(
            functools.partial(kernel, n_aux, n_pair),
            out_shape=(
                jax.ShapeDtypeStruct((8, 5), F32),
                jax.ShapeDtypeStruct((8, 1024), F32),
            ),
            in_specs=[pl.BlockSpec(memory_space=pl.ANY)] * 6,
            out_specs=[pl.BlockSpec(memory_space=pltpu.VMEM)] * 2,
            scratch_shapes=[
                tiles,
                pltpu.VMEM((1, 8), jnp.int32),
                pltpu.VMEM((1, 64), jnp.int32),
                pltpu.VMEM((256, 256), BF16),
                pltpu.VMEM((256, 256), BF16),
                pltpu.VMEM((8, 40), BF16),
                pltpu.VMEM((5, 8, 8, 1024), BF16),
                *[tiles] * 5,
                pltpu.VMEM((8, NX, 8, 256), BF16),
                pltpu.VMEM((32, 8, 256), BF16),
                pltpu.VMEM((8, 8, 128), F32),
                pltpu.VMEM((NZ, 8, 256), BF16),
                pltpu.VMEM((NX, 8, 256), F32),
                pltpu.SemaphoreType.DMA((6,)),
                *[pltpu.SemaphoreType.DMA((2, 4))] * 4,
                *[sems] * 6,
                *[pltpu.SemaphoreType.DMA((31,))] * 2,
                *[sems] * 2,
                *[pltpu.SemaphoreType.DMA((15,))] * 2,
                *[sems] * 2,
                pltpu.SemaphoreType.REGULAR((3,)),
            ],
            compiler_params=pltpu.CompilerParams(
                collective_id=0, has_side_effects=True, vmem_limit_bytes=40 << 20
            ),
        )(
            *(
                pltpu.with_memory_space_constraint(v, pltpu.HBM)
                for v in (
                    three_center,
                    tile_live,
                    pair_atoms.reshape(1, 64),
                    green_occ,
                    green_vir,
                    screened,
                )
            )
        )

    placed = (P("aux", "pair", None), P("aux", "pair"), P(), P(), P(), P("aux", None))
    return jax.shard_map(
        per_device,
        mesh=mesh,
        in_specs=placed,
        out_specs=(P("aux", "pair"), P("pair", None)),
        check_vma=False,
    )
```

```python
import functools
import math

import jax
import jax.numpy as jnp
from jax import lax
from jax.experimental import pallas as pl
from jax.experimental.pallas import tpu as pltpu
from jax.sharding import PartitionSpec as P

MESH = pl.DeviceIdType.MESH
OA = 32
NAT = 8
REACH = 2
NX = 4
NZ = 16
F32 = jnp.float32
BF16 = jnp.bfloat16


def dot(a, b, dims=((1,), (0,))):
    return lax.dot_general(a, b, (dims, ((), ())), preferred_element_type=F32)


def iota(shape, dim):
    return lax.broadcasted_iota(jnp.int32, shape, dim)


def exchange_groups(parts):
    x0, x1, x2, x3 = parts
    lane = iota(x0.shape, 1)
    low = lane < 64
    even = (lane & 32) == 0
    y0 = jnp.where(low, x0, pltpu.roll(x2, 64, 1))
    y2 = jnp.where(low, pltpu.roll(x0, 64, 1), x2)
    y1 = jnp.where(low, x1, pltpu.roll(x3, 64, 1))
    y3 = jnp.where(low, pltpu.roll(x1, 64, 1), x3)
    z0 = jnp.where(even, y0, pltpu.roll(y1, 32, 1))
    z1 = jnp.where(even, pltpu.roll(y0, 96, 1), y1)
    z2 = jnp.where(even, y2, pltpu.roll(y3, 32, 1))
    z3 = jnp.where(even, pltpu.roll(y2, 96, 1), y3)
    return z0, z1, z2, z3


def to_matrix(tiles):
    cols = [tiles[:, g * 128 : (g + 1) * 128].reshape(2, 4, 8, 128) for g in range(8)]
    parts = [
        jnp.concatenate([c[:, bl] for c in cols], axis=0).reshape(128, 128) for bl in range(4)
    ]
    out = [z.reshape(8, 2, 8, 128) for z in exchange_groups(parts)]
    halves = [
        jnp.stack([z[:, bh] for z in out], axis=1).reshape(256, 128) for bh in range(2)
    ]
    return jnp.concatenate(halves, axis=1)


def to_tiles(matrix):
    halves = [matrix[:, bh * 128 : (bh + 1) * 128].reshape(8, 4, 8, 128) for bh in range(2)]
    parts = [
        jnp.stack([h[:, r] for h in halves], axis=1).reshape(128, 128) for r in range(4)
    ]
    out = [z.reshape(8, 2, 8, 128) for z in exchange_groups(parts)]
    cols = [
        jnp.stack([z[g] for z in out], axis=1).reshape(64, 128) for g in range(8)
    ]
    return jnp.concatenate(cols, axis=1)


def rows64(value):
    return value.astype(F32).reshape(64, value.shape[-1])


def kernel(
    n_aux,
    n_pair,
    tc_hbm,
    live_hbm,
    atoms_hbm,
    occ_hbm,
    vir_hbm,
    scr_hbm,
    pol_ref,
    self_ref,
    tc,
    live,
    atoms,
    occ,
    vir,
    scr,
    win,
    mt,
    zo,
    zt,
    vo,
    vt,
    held,
    forms,
    near,
    xo,
    xr,
    chi,
    ar,
    fin,
    in_sem,
    s_win,
    r_win,
    s_far,
    r_far,
    s_m,
    r_m,
    s_z,
    r_z,
    s_v,
    r_v,
    s_x,
    r_x,
    s_c,
    r_c,
    s_a,
    r_a,
    s_f,
    r_f,
    known,
):
    a_me = lax.axis_index("aux")
    p_me = lax.axis_index("pair")
    x_me, z_me = a_me // NZ, a_me % NZ
    y_me, c_me = p_me // 2, p_me % 2
    f_me = c_me * 4 + y_me

    loads = [
        pltpu.make_async_copy(src, dst, in_sem.at[i])
        for i, (src, dst) in enumerate(
            (
                (tc_hbm, tc),
                (live_hbm, live),
                (atoms_hbm, atoms),
                (occ_hbm, occ),
                (vir_hbm, vir),
                (scr_hbm, scr),
            )
        )
    ]
    for c in loads:
        c.start()

    def by_pair(step):
        q = lax.rem(p_me + step, n_pair)
        return q, (a_me, q)

    def by_plane(step):
        q = lax.rem(p_me + step % 8, n_pair)
        x = lax.rem(x_me + step // 8, NX)
        return q, x, (x * NZ + z_me, q)

    def by_z(step):
        z = lax.rem(z_me + step, NZ)
        return z, (x_me * NZ + z, p_me)

    def by_x(step):
        x = lax.rem(x_me + step, NX)
        return x, (x * NZ + z_me, p_me)

    offsets = (1, -1)
    chunks = [pl.ds(2 * c, 2) for c in range(4)]

    def by_window(d):
        return (lax.rem(a_me + d + n_aux, n_aux), p_me)

    barrier = pltpu.get_barrier_semaphore()
    peers = [by_window(d) for d in offsets]
    peers += [by_x(step)[-1] for step in (2, 1, 3)]
    peers += [by_pair(step)[-1] for step in range(1, 8)]
    peers += [by_z(step)[-1] for step in (1, NZ - 1)]
    for device in peers:
        pl.semaphore_signal(barrier, inc=1, device_id=device, device_id_type=MESH)

    def tell(r):
        for step in (1 << r, NZ - (1 << r)):
            pl.semaphore_signal(known.at[r], inc=1, device_id=by_z(step)[-1], device_id_type=MESH)

    def hear(r):
        pl.semaphore_wait(known.at[r], 2)

    def remote(src, dst, send, recv, device):
        return pltpu.make_async_remote_copy(
            src_ref=src,
            dst_ref=dst,
            send_sem=send,
            recv_sem=recv,
            device_id=device,
            device_id_type=MESH,
        )

    def exchange(peer, count, source, dest, send, recv):
        copies = []
        for step in range(1, count):
            *there, device = peer(step)
            copies.append(remote(source(*there), dest, send.at[step - 1], recv.at[step - 1], device))
        for c in copies:
            c.start()
        return copies

    loads[0].wait()
    loads[1].wait()
    eye8 = iota((8, 8), 0) == iota((8, 8), 1)
    live_col = jnp.sum(
        jnp.where(eye8, jnp.broadcast_to(live[...].astype(F32), (8, 8)), 0.0), axis=1, keepdims=True
    )
    win[REACH] = (tc[...].astype(F32) * live_col[None]).astype(BF16)

    pl.semaphore_wait(barrier, len(peers))
    started = []
    arriving = {1: [], 3: []}
    for c, part in enumerate(chunks):
        for i, d in enumerate(offsets):
            copy = remote(
                win.at[REACH, part], win.at[REACH - d, part], s_win.at[i, c], r_win.at[i, c], by_window(d)
            )
            copy.start()
            arriving[REACH - d].append(copy)
    m_copies = exchange(
        by_pair, 8, lambda q: win.at[REACH, pl.ds(4 * (q % 2), 4)], mt.at[p_me], s_m, r_m
    )
    started += m_copies
    mt[p_me] = win[REACH, pl.ds(4 * c_me, 4)]

    for c in loads[2:]:
        c.wait()
    new = iota((256, 256), 0)
    old = iota((256, 256), 1)
    perm = jnp.where((new % 8) * 32 + new // 8 == old, 1.0, 0.0).astype(BF16)
    occ_cols = dot(occ[...], perm, ((1,), (1,))).astype(BF16)
    occ_both = dot(perm, occ_cols).astype(BF16)
    atom_row = atoms[...]
    place = iota((64, 64), 0)
    pick = jnp.where((place % 8) * 8 + place // 8 == atom_row, 1.0, 0.0).astype(BF16)
    eye64 = iota((64, 64), 0) == iota((64, 64), 1)
    atom_col = jnp.sum(
        jnp.where(eye64, jnp.broadcast_to(atom_row.astype(F32), (64, 64)), 0.0), axis=1, keepdims=True
    ).astype(jnp.int32)
    spot = iota((64, 64), 1)
    put = jnp.where((spot % 8) * 8 + spot // 8 == atom_col, 1.0, 0.0).astype(BF16)
    held[...] = jnp.broadcast_to(atom_col, (64, 128))
    own_atoms = [
        held[pl.ds(pl.multiple_of((2 * y_me + core) * 8, 8), 8), :] for core in range(2)
    ]
    second = [
        jnp.broadcast_to((v & 7)[None], (OA, 8, 128)).reshape(256, 128) for v in own_atoms
    ]
    wide_col = iota((8, 256), 1)
    firsts = [
        jnp.sum(
            jnp.where(
                iota((8, 256), 0) == wide_col % 8, jnp.concatenate([v, v], axis=1) >> 3, 0
            ).astype(F32),
            axis=0,
            keepdims=True,
        )
        for v in own_atoms
    ]
    column = iota((64, 256), 1)
    first = jnp.where((column // 64) % 2 == 0, firsts[0], firsts[1]).astype(jnp.int32)
    collect = jnp.where(
        jnp.logical_and((atom_col & 7) == (column % 64) // 8, (atom_col >> 3) == first), 1.0, 0.0
    ).astype(BF16)
    wide = jnp.broadcast_to(scr[...].astype(F32)[:, None, :], (8, 8, 40)).reshape(64, 40).astype(BF16)
    same_tile = (iota((64, 64), 0) % 8) == (iota((64, 64), 1) % 8)
    couple = []
    for slot in range(5):
        spread = jnp.where(iota((40, 64), 0) == slot * 8 + iota((40, 64), 1) // 8, 1.0, 0.0)
        block = a_me + slot - REACH
        inside = jnp.logical_and(block >= 0, block < n_aux)
        keep = jnp.logical_and(same_tile, inside)
        couple.append(jnp.where(keep, dot(wide, spread.astype(BF16)), 0.0).astype(BF16))

    tell(0)
    relayed = {0: [], 4: []}
    for c, part in enumerate(chunks):
        for i, d in enumerate(offsets):
            arriving[REACH - d][c].wait_recv()
            copy = remote(
                win.at[REACH - d, part],
                win.at[REACH - 2 * d, part],
                s_far.at[i, c],
                r_far.at[i, c],
                by_window(d),
            )
            copy.start()
            relayed[REACH - 2 * d].append(copy)
    started += arriving[1] + arriving[3] + relayed[0] + relayed[4]

    hear(0)
    tell(1)

    mixed = dot(couple[2], rows64(win[2]).astype(BF16))
    for slot in (1, 3, 0, 4):
        for c in relayed.get(slot, ()):
            c.wait_recv()
        mixed += dot(couple[slot], rows64(win[slot]).astype(BF16))
    vo[...] = mixed.reshape(8, 8, 1024).astype(BF16)
    v_copy = remote(
        vo.at[pl.ds(4 * (1 - c_me), 4)], vt.at[c_me], s_v, r_v, (a_me, y_me * 2 + 1 - c_me)
    )
    v_copy.start()
    started.append(v_copy)
    vt[c_me] = vo[pl.ds(4 * c_me, 4)]

    for c in m_copies:
        c.wait_recv()
    for i in range(4):
        form = to_matrix(dot(pick, rows64(mt[:, i]).astype(BF16))).astype(BF16)
        forms[i] = form
        near[:, i] = dot(occ_cols, form).reshape(NAT, OA, 256).astype(BF16)

    v_copy.wait_recv()
    v_form = to_matrix(rows64(vt[...]))
    stacked = []
    for core in range(2):
        half = v_form[:, core * 128 : (core + 1) * 128]
        stacked.append(
            jnp.concatenate(
                [jnp.where(second[core] == b, half, 0.0).astype(BF16) for b in range(NAT)], axis=1
            )
        )
    energy = dot(jnp.concatenate(stacked, axis=0), near[...].reshape(1024, 256))
    blocks = [to_tiles(energy[core * 256 : (core + 1) * 256]) for core in range(2)]
    upper = [v.astype(BF16) for v in blocks]
    lower = [(v - u.astype(F32)).astype(BF16) for v, u in zip(blocks, upper)]
    energy_tiles = dot(collect, jnp.concatenate(upper + lower, axis=0))
    for x in range(NX):
        xo[:, x] = energy_tiles[:, x * 256 : (x + 1) * 256].reshape(8, 8, 256).astype(BF16)
    x_copies = exchange(by_plane, 32, lambda q, x: xo.at[q, x], xr.at[x_me * 8 + p_me], s_x, r_x)
    xr[x_me * 8 + p_me] = xo[p_me, x_me]

    hear(1)
    tell(2)
    left = dot(occ_both, forms[y_me], ((0,), (0,))).astype(BF16)
    z_tiles = dot(put, to_tiles(dot(left, vir[...])).astype(BF16))
    zo[...] = z_tiles.reshape(8, 8, 1024).astype(BF16)
    z_copies = exchange(by_pair, 8, lambda q: zo.at[q], zt.at[f_me], s_z, r_z)
    started += z_copies
    zt[f_me] = zo[p_me]

    for c in x_copies:
        c.wait_recv()
    ar[z_me] = jnp.sum(xr[...].astype(F32), axis=0).astype(BF16)
    hear(2)
    a_copies = exchange(by_z, NZ, lambda z: ar.at[z_me], ar.at[z_me], s_a, r_a)

    for c in z_copies:
        c.wait_recv()
    z_rows = rows64(zt[...]).astype(BF16)
    chi_total = jnp.zeros((8, 128), F32)
    for slot in range(5):
        terms = dot(z_rows, rows64(win[slot]).astype(BF16), ((1,), (1,)))
        block = a_me + slot - REACH
        inside = jnp.logical_and(block >= 0, block < n_aux)
        keep = jnp.logical_and(same_tile, inside)
        terms = jnp.sum(jnp.where(keep, terms, 0.0).reshape(8, 8, 64), axis=1)
        gather = jnp.where(iota((64, 128), 1) == slot * 8 + iota((64, 128), 0) // 8, 1.0, 0.0)
        chi_total += jnp.dot(terms, gather, precision=lax.Precision.HIGHEST, preferred_element_type=F32)
    chi[p_me] = chi_total * (1.0 / (OA * NAT))
    c_copies = exchange(by_pair, 8, lambda q: chi.at[p_me], chi.at[p_me], s_c, r_c)
    started += c_copies

    for c in started + x_copies:
        c.wait_send()
    for c in a_copies:
        c.wait_recv()
    scale = -1.0 / math.sqrt(n_aux * 8 * NAT * OA * NAT)
    fin[x_me] = jnp.sum(ar[...].astype(F32), axis=0) * scale
    f_copies = exchange(by_x, NX, lambda x: fin.at[x_me], fin.at[x_me], s_f, r_f)

    for c in c_copies:
        c.wait_recv()
    turned = pltpu.roll(jnp.sum(chi[...], axis=0), lax.rem(128 - 5 * p_me, 128), 1)
    pol_ref[...] = turned[:, :5]
    for c in a_copies:
        c.wait_send()
    for c in f_copies:
        c.wait_recv()
    for x in range(NX):
        self_ref[:, x * 256 : (x + 1) * 256] = fin[x]
    for c in f_copies:
        c.wait_send()


def solution(mesh):
    n_aux, n_pair = mesh.shape["aux"], mesh.shape["pair"]

    def per_device(three_center, tile_live, pair_atoms, green_occ, green_vir, screened):
        tiles = pltpu.VMEM((8, 8, 1024), BF16)
        sems = pltpu.SemaphoreType.DMA((7,))
        return pl.pallas_call(
            functools.partial(kernel, n_aux, n_pair),
            out_shape=(
                jax.ShapeDtypeStruct((8, 5), F32),
                jax.ShapeDtypeStruct((8, 1024), F32),
            ),
            in_specs=[pl.BlockSpec(memory_space=pl.ANY)] * 6,
            out_specs=[pl.BlockSpec(memory_space=pltpu.VMEM)] * 2,
            scratch_shapes=[
                tiles,
                pltpu.VMEM((1, 8), jnp.int32),
                pltpu.VMEM((1, 64), jnp.int32),
                pltpu.VMEM((256, 256), BF16),
                pltpu.VMEM((256, 256), BF16),
                pltpu.VMEM((8, 40), BF16),
                pltpu.VMEM((5, 8, 8, 1024), BF16),
                pltpu.VMEM((8, 4, 8, 1024), BF16),
                *[tiles] * 3,
                pltpu.VMEM((2, 4, 8, 1024), BF16),
                pltpu.VMEM((64, 128), jnp.int32),
                pltpu.VMEM((4, 256, 256), BF16),
                pltpu.VMEM((NAT, 4, OA, 256), BF16),
                pltpu.VMEM((8, NX, 8, 256), BF16),
                pltpu.VMEM((32, 8, 256), BF16),
                pltpu.VMEM((8, 8, 128), F32),
                pltpu.VMEM((NZ, 8, 256), BF16),
                pltpu.VMEM((NX, 8, 256), F32),
                pltpu.SemaphoreType.DMA((6,)),
                *[pltpu.SemaphoreType.DMA((2, 4))] * 4,
                *[sems] * 4,
                *[pltpu.SemaphoreType.DMA(())] * 2,
                *[pltpu.SemaphoreType.DMA((31,))] * 2,
                *[sems] * 2,
                *[pltpu.SemaphoreType.DMA((15,))] * 2,
                *[sems] * 2,
                pltpu.SemaphoreType.REGULAR((3,)),
            ],
            compiler_params=pltpu.CompilerParams(
                collective_id=0, has_side_effects=True, vmem_limit_bytes=40 << 20
            ),
        )(
            *(
                pltpu.with_memory_space_constraint(v, pltpu.HBM)
                for v in (
                    three_center,
                    tile_live,
                    pair_atoms.reshape(1, 64),
                    green_occ,
                    green_vir,
                    screened,
                )
            )
        )

    placed = (P("aux", "pair", None), P("aux", "pair"), P(), P(), P(), P("aux", None))
    return jax.shard_map(
        per_device,
        mesh=mesh,
        in_specs=placed,
        out_specs=(P("aux", "pair"), P("pair", None)),
        check_vma=False,
    )
```

```python
import functools
import math

import jax
import jax.numpy as jnp
from jax import lax
from jax.experimental import pallas as pl
from jax.experimental.pallas import tpu as pltpu
from jax.sharding import PartitionSpec as P

MESH = pl.DeviceIdType.MESH
OA = 32
NAT = 8
REACH = 2
NX = 4
NZ = 16
F32 = jnp.float32
BF16 = jnp.bfloat16


def dot(a, b, dims=((1,), (0,))):
    return lax.dot_general(a, b, (dims, ((), ())), preferred_element_type=F32)


def iota(shape, dim):
    return lax.broadcasted_iota(jnp.int32, shape, dim)


def exchange_groups(parts):
    x0, x1, x2, x3 = parts
    lane = iota(x0.shape, 1)
    low = lane < 64
    even = (lane & 32) == 0
    y0 = jnp.where(low, x0, pltpu.roll(x2, 64, 1))
    y2 = jnp.where(low, pltpu.roll(x0, 64, 1), x2)
    y1 = jnp.where(low, x1, pltpu.roll(x3, 64, 1))
    y3 = jnp.where(low, pltpu.roll(x1, 64, 1), x3)
    z0 = jnp.where(even, y0, pltpu.roll(y1, 32, 1))
    z1 = jnp.where(even, pltpu.roll(y0, 96, 1), y1)
    z2 = jnp.where(even, y2, pltpu.roll(y3, 32, 1))
    z3 = jnp.where(even, pltpu.roll(y2, 96, 1), y3)
    return z0, z1, z2, z3


def to_matrix(tiles):
    cols = [tiles[:, g * 128 : (g + 1) * 128].reshape(2, 4, 8, 128) for g in range(8)]
    parts = [
        jnp.concatenate([c[:, bl] for c in cols], axis=0).reshape(128, 128) for bl in range(4)
    ]
    out = [z.reshape(8, 2, 8, 128) for z in exchange_groups(parts)]
    halves = [
        jnp.stack([z[:, bh] for z in out], axis=1).reshape(256, 128) for bh in range(2)
    ]
    return jnp.concatenate(halves, axis=1)


def to_tiles(matrix):
    halves = [matrix[:, bh * 128 : (bh + 1) * 128].reshape(8, 4, 8, 128) for bh in range(2)]
    parts = [
        jnp.stack([h[:, r] for h in halves], axis=1).reshape(128, 128) for r in range(4)
    ]
    out = [z.reshape(8, 2, 8, 128) for z in exchange_groups(parts)]
    cols = [
        jnp.stack([z[g] for z in out], axis=1).reshape(64, 128) for g in range(8)
    ]
    return jnp.concatenate(cols, axis=1)


def rows64(value):
    return value.astype(F32).reshape(64, value.shape[-1])


def kernel(
    n_aux,
    n_pair,
    tc_hbm,
    live_hbm,
    atoms_hbm,
    occ_hbm,
    vir_hbm,
    scr_hbm,
    pol_ref,
    self_ref,
    tc,
    live,
    atoms,
    occ,
    vir,
    scr,
    win,
    mt,
    zo,
    zt,
    vo,
    vt,
    held,
    forms,
    near,
    xo,
    xr,
    chi,
    ar,
    fin,
    in_sem,
    s_win,
    r_win,
    r_far,
    s_m,
    r_m,
    s_z,
    r_z,
    s_v,
    r_v,
    s_x,
    r_x,
    s_c,
    r_c,
    s_a,
    r_a,
    s_f,
    r_f,
    known,
):
    a_me = lax.axis_index("aux")
    p_me = lax.axis_index("pair")
    x_me, z_me = a_me // NZ, a_me % NZ
    y_me, c_me = p_me // 2, p_me % 2
    f_me = c_me * 4 + y_me

    loads = [
        pltpu.make_async_copy(src, dst, in_sem.at[i])
        for i, (src, dst) in enumerate(
            (
                (tc_hbm, tc),
                (live_hbm, live),
                (atoms_hbm, atoms),
                (occ_hbm, occ),
                (vir_hbm, vir),
                (scr_hbm, scr),
            )
        )
    ]
    for c in loads:
        c.start()

    def by_pair(step):
        q = lax.rem(p_me + step, n_pair)
        return q, (a_me, q)

    def by_plane(step):
        q = lax.rem(p_me + step % 8, n_pair)
        x = lax.rem(x_me + step // 8, NX)
        return q, x, (x * NZ + z_me, q)

    def by_z(step):
        z = lax.rem(z_me + step, NZ)
        return z, (x_me * NZ + z, p_me)

    def by_x(step):
        x = lax.rem(x_me + step, NX)
        return x, (x * NZ + z_me, p_me)

    offsets = (1, -1)
    chunks = [pl.ds(2 * c, 2) for c in range(4)]

    def by_window(d):
        return (lax.rem(a_me + d + n_aux, n_aux), p_me)

    barrier = pltpu.get_barrier_semaphore()
    peers = [by_window(d) for d in offsets]
    peers += [by_x(step)[-1] for step in (2, 1, 3)]
    peers += [by_pair(step)[-1] for step in range(1, 8)]
    peers += [by_z(step)[-1] for step in (1, NZ - 1)]
    for device in peers:
        pl.semaphore_signal(barrier, inc=1, device_id=device, device_id_type=MESH)

    def tell(r):
        for step in (1 << r, NZ - (1 << r)):
            pl.semaphore_signal(known.at[r], inc=1, device_id=by_z(step)[-1], device_id_type=MESH)

    def hear(r):
        pl.semaphore_wait(known.at[r], 2)

    def remote(src, dst, send, recv, device):
        return pltpu.make_async_remote_copy(
            src_ref=src,
            dst_ref=dst,
            send_sem=send,
            recv_sem=recv,
            device_id=device,
            device_id_type=MESH,
        )

    def exchange(peer, count, source, dest, send, recv):
        for step in sorted(range(1, count), key=lambda v: distance(peer, v)):
            *there, device = peer(step)
            remote(source(*there), dest, send, recv, device).start()

    def distance(peer, step):
        if peer is by_plane:
            return abs(step % 8 - 4) + 2 * abs(step // 8 - 2)
        return abs(step - {by_pair: 4, by_z: NZ // 2, by_x: 2}[peer])

    def await_all(slots, sem):
        pltpu.make_async_copy(slots, slots, sem).wait()

    loads[0].wait()
    loads[1].wait()
    eye8 = iota((8, 8), 0) == iota((8, 8), 1)
    live_col = jnp.sum(
        jnp.where(eye8, jnp.broadcast_to(live[...].astype(F32), (8, 8)), 0.0), axis=1, keepdims=True
    )
    win[REACH] = (tc[...].astype(F32) * live_col[None]).astype(BF16)

    pl.semaphore_wait(barrier, len(peers))
    arriving = {1: [], 3: []}
    for c, part in enumerate(chunks):
        for i, d in enumerate(offsets):
            copy = remote(
                win.at[REACH, part], win.at[REACH - d, part], s_win, r_win.at[i, c], by_window(d)
            )
            copy.start()
            arriving[REACH - d].append(copy)
    exchange(
        by_pair, 8, lambda q: win.at[REACH, pl.ds(4 * (q % 2), 4)], mt.at[p_me], s_m, r_m
    )
    mt[p_me] = win[REACH, pl.ds(4 * c_me, 4)]

    for c in loads[2:]:
        c.wait()
    new = iota((256, 256), 0)
    old = iota((256, 256), 1)
    perm = jnp.where((new % 8) * 32 + new // 8 == old, 1.0, 0.0).astype(BF16)
    occ_cols = dot(occ[...], perm, ((1,), (1,))).astype(BF16)
    occ_both = dot(perm, occ_cols).astype(BF16)
    atom_row = atoms[...]
    place = iota((64, 64), 0)
    pick = jnp.where((place % 8) * 8 + place // 8 == atom_row, 1.0, 0.0).astype(BF16)
    eye64 = iota((64, 64), 0) == iota((64, 64), 1)
    atom_col = jnp.sum(
        jnp.where(eye64, jnp.broadcast_to(atom_row.astype(F32), (64, 64)), 0.0), axis=1, keepdims=True
    ).astype(jnp.int32)
    spot = iota((64, 64), 1)
    put = jnp.where((spot % 8) * 8 + spot // 8 == atom_col, 1.0, 0.0).astype(BF16)
    held[...] = jnp.broadcast_to(atom_col, (64, 128))
    own_atoms = [
        held[pl.ds(pl.multiple_of((2 * y_me + core) * 8, 8), 8), :] for core in range(2)
    ]
    second = [
        jnp.broadcast_to((v & 7)[None], (OA, 8, 128)).reshape(256, 128) for v in own_atoms
    ]
    wide_col = iota((8, 256), 1)
    firsts = [
        jnp.sum(
            jnp.where(
                iota((8, 256), 0) == wide_col % 8, jnp.concatenate([v, v], axis=1) >> 3, 0
            ).astype(F32),
            axis=0,
            keepdims=True,
        )
        for v in own_atoms
    ]
    column = iota((64, 256), 1)
    first = jnp.where((column // 64) % 2 == 0, firsts[0], firsts[1]).astype(jnp.int32)
    collect = jnp.where(
        jnp.logical_and((atom_col & 7) == (column % 64) // 8, (atom_col >> 3) == first), 1.0, 0.0
    ).astype(BF16)
    wide = jnp.broadcast_to(scr[...].astype(F32)[:, None, :], (8, 8, 40)).reshape(64, 40).astype(BF16)
    same_tile = (iota((64, 64), 0) % 8) == (iota((64, 64), 1) % 8)
    couple = []
    for slot in range(5):
        spread = jnp.where(iota((40, 64), 0) == slot * 8 + iota((40, 64), 1) // 8, 1.0, 0.0)
        block = a_me + slot - REACH
        inside = jnp.logical_and(block >= 0, block < n_aux)
        keep = jnp.logical_and(same_tile, inside)
        couple.append(jnp.where(keep, dot(wide, spread.astype(BF16)), 0.0).astype(BF16))

    tell(0)
    for c, part in enumerate(chunks):
        for i, d in enumerate(offsets):
            arriving[REACH - d][c].wait_recv()
            copy = remote(
                win.at[REACH - d, part],
                win.at[REACH - 2 * d, part],
                s_win,
                r_far.at[i],
                by_window(d),
            )
            copy.start()
    hear(0)
    tell(1)

    mixed = dot(couple[2], rows64(win[2]).astype(BF16))
    for slot in (1, 3, 0, 4):
        if slot in (0, 4):
            await_all(win.at[slot], r_far.at[slot // 4])
        mixed += dot(couple[slot], rows64(win[slot]).astype(BF16))
    vo[...] = mixed.reshape(8, 8, 1024).astype(BF16)
    v_copy = remote(
        vo.at[pl.ds(4 * (1 - c_me), 4)], vt.at[c_me], s_v, r_v, (a_me, y_me * 2 + 1 - c_me)
    )
    v_copy.start()
    vt[c_me] = vo[pl.ds(4 * c_me, 4)]

    await_all(mt.at[pl.ds(0, 7)], r_m)
    for i in range(4):
        form = to_matrix(dot(pick, rows64(mt[:, i]).astype(BF16))).astype(BF16)
        forms[i] = form
        near[:, i] = dot(occ_cols, form).reshape(NAT, OA, 256).astype(BF16)

    v_copy.wait_recv()
    v_form = to_matrix(rows64(vt[...]))
    stacked = []
    for core in range(2):
        half = v_form[:, core * 128 : (core + 1) * 128]
        stacked.append(
            jnp.concatenate(
                [jnp.where(second[core] == b, half, 0.0).astype(BF16) for b in range(NAT)], axis=1
            )
        )
    energy = dot(jnp.concatenate(stacked, axis=0), near[...].reshape(1024, 256))
    blocks = [to_tiles(energy[core * 256 : (core + 1) * 256]) for core in range(2)]
    upper = [v.astype(BF16) for v in blocks]
    lower = [(v - u.astype(F32)).astype(BF16) for v, u in zip(blocks, upper)]
    energy_tiles = dot(collect, jnp.concatenate(upper + lower, axis=0))
    for x in range(NX):
        xo[:, x] = energy_tiles[:, x * 256 : (x + 1) * 256].reshape(8, 8, 256).astype(BF16)
    exchange(by_plane, 32, lambda q, x: xo.at[q, x], xr.at[x_me * 8 + p_me], s_x, r_x)
    xr[x_me * 8 + p_me] = xo[p_me, x_me]

    hear(1)
    tell(2)
    left = dot(occ_both, forms[y_me], ((0,), (0,))).astype(BF16)
    z_tiles = dot(put, to_tiles(dot(left, vir[...])).astype(BF16))
    zo[...] = z_tiles.reshape(8, 8, 1024).astype(BF16)
    exchange(by_pair, 8, lambda q: zo.at[q], zt.at[f_me], s_z, r_z)
    zt[f_me] = zo[p_me]

    await_all(xr.at[pl.ds(0, 31)], r_x)
    ar[z_me] = jnp.sum(xr[...].astype(F32), axis=0).astype(BF16)
    hear(2)
    exchange(by_z, NZ, lambda z: ar.at[z_me], ar.at[z_me], s_a, r_a)

    await_all(zt.at[pl.ds(0, 7)], r_z)
    z_rows = rows64(zt[...]).astype(BF16)
    chi_total = jnp.zeros((8, 128), F32)
    for slot in range(5):
        terms = dot(z_rows, rows64(win[slot]).astype(BF16), ((1,), (1,)))
        block = a_me + slot - REACH
        inside = jnp.logical_and(block >= 0, block < n_aux)
        keep = jnp.logical_and(same_tile, inside)
        terms = jnp.sum(jnp.where(keep, terms, 0.0).reshape(8, 8, 64), axis=1)
        gather = jnp.where(iota((64, 128), 1) == slot * 8 + iota((64, 128), 0) // 8, 1.0, 0.0)
        chi_total += jnp.dot(terms, gather, precision=lax.Precision.HIGHEST, preferred_element_type=F32)
    chi[p_me] = chi_total * (1.0 / (OA * NAT))
    exchange(by_pair, 8, lambda q: chi.at[p_me], chi.at[p_me], s_c, r_c)

    await_all(win.at[pl.ds(0, 4)], s_win)
    await_all(mt.at[pl.ds(0, 7)], s_m)
    v_copy.wait_send()
    await_all(zt.at[pl.ds(0, 7)], s_z)
    await_all(xr.at[pl.ds(0, 31)], s_x)
    await_all(ar.at[pl.ds(0, NZ - 1)], r_a)
    scale = -1.0 / math.sqrt(n_aux * 8 * NAT * OA * NAT)
    fin[x_me] = jnp.sum(ar[...].astype(F32), axis=0) * scale
    exchange(by_x, NX, lambda x: fin.at[x_me], fin.at[x_me], s_f, r_f)

    await_all(chi.at[pl.ds(0, 7)], r_c)
    turned = pltpu.roll(jnp.sum(chi[...], axis=0), lax.rem(128 - 5 * p_me, 128), 1)
    pol_ref[...] = turned[:, :5]
    await_all(ar.at[pl.ds(0, NZ - 1)], s_a)
    await_all(chi.at[pl.ds(0, 7)], s_c)
    await_all(fin.at[pl.ds(0, NX - 1)], r_f)
    for x in range(NX):
        self_ref[:, x * 256 : (x + 1) * 256] = fin[x]
    await_all(fin.at[pl.ds(0, NX - 1)], s_f)


def solution(mesh):
    n_aux, n_pair = mesh.shape["aux"], mesh.shape["pair"]

    def per_device(three_center, tile_live, pair_atoms, green_occ, green_vir, screened):
        tiles = pltpu.VMEM((8, 8, 1024), BF16)
        return pl.pallas_call(
            functools.partial(kernel, n_aux, n_pair),
            out_shape=(
                jax.ShapeDtypeStruct((8, 5), F32),
                jax.ShapeDtypeStruct((8, 1024), F32),
            ),
            in_specs=[pl.BlockSpec(memory_space=pl.ANY)] * 6,
            out_specs=[pl.BlockSpec(memory_space=pltpu.VMEM)] * 2,
            scratch_shapes=[
                tiles,
                pltpu.VMEM((1, 8), jnp.int32),
                pltpu.VMEM((1, 64), jnp.int32),
                pltpu.VMEM((256, 256), BF16),
                pltpu.VMEM((256, 256), BF16),
                pltpu.VMEM((8, 40), BF16),
                pltpu.VMEM((5, 8, 8, 1024), BF16),
                pltpu.VMEM((8, 4, 8, 1024), BF16),
                *[tiles] * 3,
                pltpu.VMEM((2, 4, 8, 1024), BF16),
                pltpu.VMEM((64, 128), jnp.int32),
                pltpu.VMEM((4, 256, 256), BF16),
                pltpu.VMEM((NAT, 4, OA, 256), BF16),
                pltpu.VMEM((8, NX, 8, 256), BF16),
                pltpu.VMEM((32, 8, 256), BF16),
                pltpu.VMEM((8, 8, 128), F32),
                pltpu.VMEM((NZ, 8, 256), BF16),
                pltpu.VMEM((NX, 8, 256), F32),
                pltpu.SemaphoreType.DMA((6,)),
                pltpu.SemaphoreType.DMA(()),
                pltpu.SemaphoreType.DMA((2, 4)),
                pltpu.SemaphoreType.DMA((2,)),
                *[pltpu.SemaphoreType.DMA(())] * 14,
                pltpu.SemaphoreType.REGULAR((3,)),
            ],
            compiler_params=pltpu.CompilerParams(
                collective_id=0, has_side_effects=True, vmem_limit_bytes=40 << 20
            ),
        )(
            *(
                pltpu.with_memory_space_constraint(v, pltpu.HBM)
                for v in (
                    three_center,
                    tile_live,
                    pair_atoms.reshape(1, 64),
                    green_occ,
                    green_vir,
                    screened,
                )
            )
        )

    placed = (P("aux", "pair", None), P("aux", "pair"), P(), P(), P(), P("aux", None))
    return jax.shard_map(
        per_device,
        mesh=mesh,
        in_specs=placed,
        out_specs=(P("aux", "pair"), P("pair", None)),
        check_vma=False,
    )
```

```python
import functools
import math

import jax
import jax.numpy as jnp
from jax import lax
from jax.experimental import pallas as pl
from jax.experimental.pallas import tpu as pltpu
from jax.sharding import PartitionSpec as P

MESH = pl.DeviceIdType.MESH
OA = 32
NAT = 8
REACH = 2
NX = 4
NZ = 16
F32 = jnp.float32
BF16 = jnp.bfloat16


def dot(a, b, dims=((1,), (0,))):
    return lax.dot_general(a, b, (dims, ((), ())), preferred_element_type=F32)


def iota(shape, dim):
    return lax.broadcasted_iota(jnp.int32, shape, dim)


def exchange_groups(parts):
    x0, x1, x2, x3 = parts
    lane = iota(x0.shape, 1)
    low = lane < 64
    even = (lane & 32) == 0
    y0 = jnp.where(low, x0, pltpu.roll(x2, 64, 1))
    y2 = jnp.where(low, pltpu.roll(x0, 64, 1), x2)
    y1 = jnp.where(low, x1, pltpu.roll(x3, 64, 1))
    y3 = jnp.where(low, pltpu.roll(x1, 64, 1), x3)
    z0 = jnp.where(even, y0, pltpu.roll(y1, 32, 1))
    z1 = jnp.where(even, pltpu.roll(y0, 96, 1), y1)
    z2 = jnp.where(even, y2, pltpu.roll(y3, 32, 1))
    z3 = jnp.where(even, pltpu.roll(y2, 96, 1), y3)
    return z0, z1, z2, z3


def to_matrix(tiles):
    cols = [tiles[:, g * 128 : (g + 1) * 128].reshape(2, 4, 8, 128) for g in range(8)]
    parts = [
        jnp.concatenate([c[:, bl] for c in cols], axis=0).reshape(128, 128) for bl in range(4)
    ]
    out = [z.reshape(8, 2, 8, 128) for z in exchange_groups(parts)]
    halves = [
        jnp.stack([z[:, bh] for z in out], axis=1).reshape(256, 128) for bh in range(2)
    ]
    return jnp.concatenate(halves, axis=1)


def to_tiles(matrix):
    halves = [matrix[:, bh * 128 : (bh + 1) * 128].reshape(8, 4, 8, 128) for bh in range(2)]
    parts = [
        jnp.stack([h[:, r] for h in halves], axis=1).reshape(128, 128) for r in range(4)
    ]
    out = [z.reshape(8, 2, 8, 128) for z in exchange_groups(parts)]
    cols = [
        jnp.stack([z[g] for z in out], axis=1).reshape(64, 128) for g in range(8)
    ]
    return jnp.concatenate(cols, axis=1)


def rows64(value):
    return value.astype(F32).reshape(64, value.shape[-1])


def kernel(
    n_aux,
    n_pair,
    tc_hbm,
    live_hbm,
    atoms_hbm,
    occ_hbm,
    vir_hbm,
    scr_hbm,
    pol_ref,
    self_ref,
    tc,
    live,
    atoms,
    occ,
    vir,
    scr,
    win,
    mt,
    zo,
    zt,
    vo,
    vt,
    held,
    forms,
    near,
    xo,
    xr,
    chi,
    ar,
    fin,
    in_sem,
    s_win,
    r_win,
    r_far,
    s_m,
    r_m,
    s_z,
    r_z,
    s_v,
    r_v,
    s_x,
    r_x,
    s_c,
    r_c,
    s_a,
    r_a,
    s_f,
    r_f,
    known,
):
    a_me = lax.axis_index("aux")
    p_me = lax.axis_index("pair")
    x_me, z_me = a_me // NZ, a_me % NZ
    y_me, c_me = p_me // 2, p_me % 2
    f_me = c_me * 4 + y_me

    def by_pair(step):
        q = lax.rem(p_me + step, n_pair)
        return q, (a_me, q)

    def by_plane(step):
        q = lax.rem(p_me + step % 8, n_pair)
        x = lax.rem(x_me + step // 8, NX)
        return q, x, (x * NZ + z_me, q)

    def by_z(step):
        z = lax.rem(z_me + step, NZ)
        return z, (x_me * NZ + z, p_me)

    def by_x(step):
        x = lax.rem(x_me + step, NX)
        return x, (x * NZ + z_me, p_me)

    offsets = (1, -1)
    chunks = [pl.ds(2 * c, 2) for c in range(4)]

    def by_window(d):
        return (lax.rem(a_me + d + n_aux, n_aux), p_me)

    barrier = pltpu.get_barrier_semaphore()
    peers = [by_window(d) for d in offsets]
    peers += [by_x(step)[-1] for step in (2, 1, 3)]
    peers += [by_pair(step)[-1] for step in range(1, 8)]
    peers += [by_z(step)[-1] for step in (1, NZ - 1)]
    for device in peers:
        pl.semaphore_signal(barrier, inc=1, device_id=device, device_id_type=MESH)

    loads = [
        pltpu.make_async_copy(src, dst, in_sem.at[i])
        for i, (src, dst) in enumerate(
            (
                (tc_hbm, tc),
                (live_hbm, live),
                (atoms_hbm, atoms),
                (occ_hbm, occ),
                (vir_hbm, vir),
                (scr_hbm, scr),
            )
        )
    ]
    for c in loads:
        c.start()

    def tell(r):
        for step in (1 << r, NZ - (1 << r)):
            pl.semaphore_signal(known.at[r], inc=1, device_id=by_z(step)[-1], device_id_type=MESH)

    def hear(r):
        pl.semaphore_wait(known.at[r], 2)

    def remote(src, dst, send, recv, device):
        return pltpu.make_async_remote_copy(
            src_ref=src,
            dst_ref=dst,
            send_sem=send,
            recv_sem=recv,
            device_id=device,
            device_id_type=MESH,
        )

    def exchange(peer, count, source, dest, send, recv):
        for step in sorted(range(1, count), key=lambda v: distance(peer, v)):
            *there, device = peer(step)
            remote(source(*there), dest, send, recv, device).start()

    def distance(peer, step):
        if peer is by_plane:
            return abs(step % 8 - 4) + 2 * abs(step // 8 - 2)
        return abs(step - {by_pair: 4, by_z: NZ // 2, by_x: 2}[peer])

    def await_all(slots, sem):
        pltpu.make_async_copy(slots, slots, sem).wait()

    loads[0].wait()
    loads[1].wait()
    eye8 = iota((8, 8), 0) == iota((8, 8), 1)
    live_col = jnp.sum(
        jnp.where(eye8, jnp.broadcast_to(live[...].astype(F32), (8, 8)), 0.0), axis=1, keepdims=True
    )
    win[REACH] = (tc[...].astype(F32) * live_col[None]).astype(BF16)

    pl.semaphore_wait(barrier, len(peers))
    arriving = {1: [], 3: []}
    for c, part in enumerate(chunks):
        for i, d in enumerate(offsets):
            copy = remote(
                win.at[REACH, part], win.at[REACH - d, part], s_win, r_win.at[i, c], by_window(d)
            )
            copy.start()
            arriving[REACH - d].append(copy)
    for h in range(2):
        exchange(
            by_pair,
            8,
            lambda q: win.at[REACH, pl.ds(4 * (q % 2) + 2 * h, 2)],
            mt.at[h, p_me],
            s_m,
            r_m.at[h],
        )
        mt[h, p_me] = win[REACH, pl.ds(4 * c_me + 2 * h, 2)]

    for c in loads[2:]:
        c.wait()
    new = iota((256, 256), 0)
    old = iota((256, 256), 1)
    perm = jnp.where((new % 8) * 32 + new // 8 == old, 1.0, 0.0).astype(BF16)
    occ_cols = dot(occ[...], perm, ((1,), (1,))).astype(BF16)
    occ_both = dot(perm, occ_cols).astype(BF16)
    atom_row = atoms[...]
    place = iota((64, 64), 0)
    pick = jnp.where((place % 8) * 8 + place // 8 == atom_row, 1.0, 0.0).astype(BF16)
    eye64 = iota((64, 64), 0) == iota((64, 64), 1)
    atom_col = jnp.sum(
        jnp.where(eye64, jnp.broadcast_to(atom_row.astype(F32), (64, 64)), 0.0), axis=1, keepdims=True
    ).astype(jnp.int32)
    spot = iota((64, 64), 1)
    put = jnp.where((spot % 8) * 8 + spot // 8 == atom_col, 1.0, 0.0).astype(BF16)
    held[...] = jnp.broadcast_to(atom_col, (64, 128))
    own_atoms = [
        held[pl.ds(pl.multiple_of((2 * y_me + core) * 8, 8), 8), :] for core in range(2)
    ]
    second = [
        jnp.broadcast_to((v & 7)[None], (OA, 8, 128)).reshape(256, 128) for v in own_atoms
    ]
    wide_col = iota((8, 256), 1)
    firsts = [
        jnp.sum(
            jnp.where(
                iota((8, 256), 0) == wide_col % 8, jnp.concatenate([v, v], axis=1) >> 3, 0
            ).astype(F32),
            axis=0,
            keepdims=True,
        )
        for v in own_atoms
    ]
    column = iota((64, 256), 1)
    first = jnp.where((column // 64) % 2 == 0, firsts[0], firsts[1]).astype(jnp.int32)
    collect = jnp.where(
        jnp.logical_and((atom_col & 7) == (column % 64) // 8, (atom_col >> 3) == first), 1.0, 0.0
    ).astype(BF16)
    wide = jnp.broadcast_to(scr[...].astype(F32)[:, None, :], (8, 8, 40)).reshape(64, 40).astype(BF16)
    same_tile = (iota((64, 64), 0) % 8) == (iota((64, 64), 1) % 8)
    couple = []
    for slot in range(5):
        spread = jnp.where(iota((40, 64), 0) == slot * 8 + iota((40, 64), 1) // 8, 1.0, 0.0)
        block = a_me + slot - REACH
        inside = jnp.logical_and(block >= 0, block < n_aux)
        keep = jnp.logical_and(same_tile, inside)
        couple.append(jnp.where(keep, dot(wide, spread.astype(BF16)), 0.0).astype(BF16))

    tell(0)
    for c, part in enumerate(chunks):
        for i, d in enumerate(offsets):
            arriving[REACH - d][c].wait_recv()
            copy = remote(
                win.at[REACH - d, part],
                win.at[REACH - 2 * d, part],
                s_win,
                r_far.at[i],
                by_window(d),
            )
            copy.start()
    hear(0)
    tell(1)

    def n_half(h):
        await_all(mt.at[h, pl.ds(0, 7)], r_m.at[h])
        for i in range(2):
            form = to_matrix(dot(pick, rows64(mt[h, :, i]).astype(BF16))).astype(BF16)
            forms[2 * h + i] = form
            near[:, 2 * h + i] = dot(occ_cols, form).reshape(NAT, OA, 256).astype(BF16)

    mixed = dot(couple[2], rows64(win[2]).astype(BF16))
    for slot in (1, 3, 0, 4):
        if slot == 0:
            n_half(0)
        if slot in (0, 4):
            await_all(win.at[slot], r_far.at[slot // 4])
        mixed += dot(couple[slot], rows64(win[slot]).astype(BF16))
    vo[...] = mixed.reshape(8, 8, 1024).astype(BF16)
    v_copy = remote(
        vo.at[pl.ds(4 * (1 - c_me), 4)], vt.at[c_me], s_v, r_v, (a_me, y_me * 2 + 1 - c_me)
    )
    v_copy.start()
    vt[c_me] = vo[pl.ds(4 * c_me, 4)]

    n_half(1)

    v_copy.wait_recv()
    v_form = to_matrix(rows64(vt[...]))
    stacked = []
    for core in range(2):
        half = v_form[:, core * 128 : (core + 1) * 128]
        stacked.append(
            jnp.concatenate(
                [jnp.where(second[core] == b, half, 0.0).astype(BF16) for b in range(NAT)], axis=1
            )
        )
    energy = dot(jnp.concatenate(stacked, axis=0), near[...].reshape(1024, 256))
    blocks = [to_tiles(energy[core * 256 : (core + 1) * 256]) for core in range(2)]
    upper = [v.astype(BF16) for v in blocks]
    lower = [(v - u.astype(F32)).astype(BF16) for v, u in zip(blocks, upper)]
    energy_tiles = dot(collect, jnp.concatenate(upper + lower, axis=0))
    for x in range(NX):
        xo[:, x] = energy_tiles[:, x * 256 : (x + 1) * 256].reshape(8, 8, 256).astype(BF16)
    exchange(by_plane, 32, lambda q, x: xo.at[q, x], xr.at[x_me * 8 + p_me], s_x, r_x)
    xr[x_me * 8 + p_me] = xo[p_me, x_me]

    hear(1)
    tell(2)
    left = dot(occ_both, forms[y_me], ((0,), (0,))).astype(BF16)
    z_tiles = dot(put, to_tiles(dot(left, vir[...])).astype(BF16))
    zo[...] = z_tiles.reshape(8, 8, 1024).astype(BF16)
    exchange(by_pair, 8, lambda q: zo.at[q], zt.at[f_me], s_z, r_z)
    zt[f_me] = zo[p_me]

    await_all(xr.at[pl.ds(0, 31)], r_x)
    ar[z_me] = jnp.sum(xr[...].astype(F32), axis=0).astype(BF16)
    hear(2)
    exchange(by_z, NZ, lambda z: ar.at[z_me], ar.at[z_me], s_a, r_a)

    await_all(zt.at[pl.ds(0, 7)], r_z)
    z_rows = rows64(zt[...]).astype(BF16)
    chi_total = jnp.zeros((8, 128), F32)
    for slot in range(5):
        terms = dot(z_rows, rows64(win[slot]).astype(BF16), ((1,), (1,)))
        block = a_me + slot - REACH
        inside = jnp.logical_and(block >= 0, block < n_aux)
        keep = jnp.logical_and(same_tile, inside)
        terms = jnp.sum(jnp.where(keep, terms, 0.0).reshape(8, 8, 64), axis=1)
        gather = jnp.where(iota((64, 128), 1) == slot * 8 + iota((64, 128), 0) // 8, 1.0, 0.0)
        chi_total += jnp.dot(terms, gather, precision=lax.Precision.HIGHEST, preferred_element_type=F32)
    chi[p_me] = chi_total * (1.0 / (OA * NAT))
    exchange(by_pair, 8, lambda q: chi.at[p_me], chi.at[p_me], s_c, r_c)

    await_all(win.at[pl.ds(0, 4)], s_win)
    await_all(mt.at[:, pl.ds(0, 7)], s_m)
    v_copy.wait_send()
    await_all(zt.at[pl.ds(0, 7)], s_z)
    await_all(xr.at[pl.ds(0, 31)], s_x)
    await_all(ar.at[pl.ds(0, NZ - 1)], r_a)
    scale = -1.0 / math.sqrt(n_aux * 8 * NAT * OA * NAT)
    fin[x_me] = jnp.sum(ar[...].astype(F32), axis=0) * scale
    exchange(by_x, NX, lambda x: fin.at[x_me], fin.at[x_me], s_f, r_f)

    await_all(chi.at[pl.ds(0, 7)], r_c)
    turned = pltpu.roll(jnp.sum(chi[...], axis=0), lax.rem(128 - 5 * p_me, 128), 1)
    pol_ref[...] = turned[:, :5]
    await_all(ar.at[pl.ds(0, NZ - 1)], s_a)
    await_all(chi.at[pl.ds(0, 7)], s_c)
    await_all(fin.at[pl.ds(0, NX - 1)], r_f)
    for x in range(NX):
        self_ref[:, x * 256 : (x + 1) * 256] = fin[x]
    await_all(fin.at[pl.ds(0, NX - 1)], s_f)


def solution(mesh):
    n_aux, n_pair = mesh.shape["aux"], mesh.shape["pair"]

    def per_device(three_center, tile_live, pair_atoms, green_occ, green_vir, screened):
        tiles = pltpu.VMEM((8, 8, 1024), BF16)
        return pl.pallas_call(
            functools.partial(kernel, n_aux, n_pair),
            out_shape=(
                jax.ShapeDtypeStruct((8, 5), F32),
                jax.ShapeDtypeStruct((8, 1024), F32),
            ),
            in_specs=[pl.BlockSpec(memory_space=pl.ANY)] * 6,
            out_specs=[pl.BlockSpec(memory_space=pltpu.VMEM)] * 2,
            scratch_shapes=[
                tiles,
                pltpu.VMEM((1, 8), jnp.int32),
                pltpu.VMEM((1, 64), jnp.int32),
                pltpu.VMEM((256, 256), BF16),
                pltpu.VMEM((256, 256), BF16),
                pltpu.VMEM((8, 40), BF16),
                pltpu.VMEM((5, 8, 8, 1024), BF16),
                pltpu.VMEM((2, 8, 2, 8, 1024), BF16),
                *[tiles] * 3,
                pltpu.VMEM((2, 4, 8, 1024), BF16),
                pltpu.VMEM((64, 128), jnp.int32),
                pltpu.VMEM((4, 256, 256), BF16),
                pltpu.VMEM((NAT, 4, OA, 256), BF16),
                pltpu.VMEM((8, NX, 8, 256), BF16),
                pltpu.VMEM((32, 8, 256), BF16),
                pltpu.VMEM((8, 8, 128), F32),
                pltpu.VMEM((NZ, 8, 256), BF16),
                pltpu.VMEM((NX, 8, 256), F32),
                pltpu.SemaphoreType.DMA((6,)),
                pltpu.SemaphoreType.DMA(()),
                pltpu.SemaphoreType.DMA((2, 4)),
                pltpu.SemaphoreType.DMA((2,)),
                pltpu.SemaphoreType.DMA(()),
                pltpu.SemaphoreType.DMA((2,)),
                *[pltpu.SemaphoreType.DMA(())] * 12,
                pltpu.SemaphoreType.REGULAR((3,)),
            ],
            compiler_params=pltpu.CompilerParams(
                collective_id=0, has_side_effects=True, vmem_limit_bytes=40 << 20
            ),
        )(
            *(
                pltpu.with_memory_space_constraint(v, pltpu.HBM)
                for v in (
                    three_center,
                    tile_live,
                    pair_atoms.reshape(1, 64),
                    green_occ,
                    green_vir,
                    screened,
                )
            )
        )

    placed = (P("aux", "pair", None), P("aux", "pair"), P(), P(), P(), P("aux", None))
    return jax.shard_map(
        per_device,
        mesh=mesh,
        in_specs=placed,
        out_specs=(P("aux", "pair"), P("pair", None)),
        check_vma=False,
    )
```

```python
import functools
import math

import jax
import jax.numpy as jnp
from jax import lax
from jax.experimental import pallas as pl
from jax.experimental.pallas import tpu as pltpu
from jax.sharding import PartitionSpec as P

MESH = pl.DeviceIdType.MESH
OA = 32
NAT = 8
REACH = 2
NX = 4
NZ = 16
F32 = jnp.float32
BF16 = jnp.bfloat16


def dot(a, b, dims=((1,), (0,))):
    return lax.dot_general(a, b, (dims, ((), ())), preferred_element_type=F32)


def iota(shape, dim):
    return lax.broadcasted_iota(jnp.int32, shape, dim)


def exchange_groups(parts):
    x0, x1, x2, x3 = parts
    lane = iota(x0.shape, 1)
    low = lane < 64
    even = (lane & 32) == 0
    y0 = jnp.where(low, x0, pltpu.roll(x2, 64, 1))
    y2 = jnp.where(low, pltpu.roll(x0, 64, 1), x2)
    y1 = jnp.where(low, x1, pltpu.roll(x3, 64, 1))
    y3 = jnp.where(low, pltpu.roll(x1, 64, 1), x3)
    z0 = jnp.where(even, y0, pltpu.roll(y1, 32, 1))
    z1 = jnp.where(even, pltpu.roll(y0, 96, 1), y1)
    z2 = jnp.where(even, y2, pltpu.roll(y3, 32, 1))
    z3 = jnp.where(even, pltpu.roll(y2, 96, 1), y3)
    return z0, z1, z2, z3


def to_matrix(tiles):
    cols = [tiles[:, g * 128 : (g + 1) * 128].reshape(2, 4, 8, 128) for g in range(8)]
    parts = [
        jnp.concatenate([c[:, bl] for c in cols], axis=0).reshape(128, 128) for bl in range(4)
    ]
    out = [z.reshape(8, 2, 8, 128) for z in exchange_groups(parts)]
    halves = [
        jnp.stack([z[:, bh] for z in out], axis=1).reshape(256, 128) for bh in range(2)
    ]
    return jnp.concatenate(halves, axis=1)


def to_tiles(matrix):
    halves = [matrix[:, bh * 128 : (bh + 1) * 128].reshape(8, 4, 8, 128) for bh in range(2)]
    parts = [
        jnp.stack([h[:, r] for h in halves], axis=1).reshape(128, 128) for r in range(4)
    ]
    out = [z.reshape(8, 2, 8, 128) for z in exchange_groups(parts)]
    cols = [
        jnp.stack([z[g] for z in out], axis=1).reshape(64, 128) for g in range(8)
    ]
    return jnp.concatenate(cols, axis=1)


def rows64(value):
    return value.astype(F32).reshape(64, value.shape[-1])


def kernel(
    n_aux,
    n_pair,
    tc_hbm,
    live_hbm,
    atoms_hbm,
    occ_hbm,
    vir_hbm,
    scr_hbm,
    pol_ref,
    self_ref,
    tc,
    live,
    atoms,
    occ,
    vir,
    scr,
    win,
    mt,
    zo,
    zt,
    vo,
    vt,
    held,
    forms,
    near,
    xo,
    xr,
    chi,
    ar,
    both,
    fin,
    in_sem,
    s_win,
    r_win,
    r_far,
    s_m,
    r_m,
    s_z,
    r_z,
    s_v,
    r_v,
    s_x,
    r_x,
    s_c,
    r_c,
    s_a,
    r_a,
    s_f,
    r_f,
    known,
):
    a_me = lax.axis_index("aux")
    p_me = lax.axis_index("pair")
    x_me, z_me = a_me // NZ, a_me % NZ
    y_me, c_me = p_me // 2, p_me % 2
    f_me = c_me * 4 + y_me

    def by_pair(step):
        q = lax.rem(p_me + step, n_pair)
        return q, (a_me, q)

    def by_chip(step):
        x = lax.rem(x_me + step // 4, NX)
        y = lax.rem(y_me + step % 4, 4)
        return y, x, (x * NZ + z_me, y * 2 + 1)

    def by_z(step):
        z = lax.rem(z_me + step, NZ)
        return z, (x_me * NZ + z, p_me)

    def by_x(step):
        x = lax.rem(x_me + step, NX)
        return x, (x * NZ + z_me, p_me)

    offsets = (1, -1)
    chunks = [pl.ds(2 * c, 2) for c in range(4)]

    def by_window(d):
        return (lax.rem(a_me + d + n_aux, n_aux), p_me)

    barrier = pltpu.get_barrier_semaphore()
    peers = [by_window(d) for d in offsets]
    peers += [by_x(step)[-1] for step in (2, 1, 3)]
    peers += [by_pair(step)[-1] for step in range(1, 8)]
    peers += [by_z(step)[-1] for step in (1, NZ - 1)]
    for device in peers:
        pl.semaphore_signal(barrier, inc=1, device_id=device, device_id_type=MESH)

    loads = [
        pltpu.make_async_copy(src, dst, in_sem.at[i])
        for i, (src, dst) in enumerate(
            (
                (tc_hbm, tc),
                (live_hbm, live),
                (atoms_hbm, atoms),
                (occ_hbm, occ),
                (vir_hbm, vir),
                (scr_hbm, scr),
            )
        )
    ]
    for c in loads:
        c.start()

    def tell(r):
        for step in (1 << r, NZ - (1 << r)):
            pl.semaphore_signal(known.at[r], inc=1, device_id=by_z(step)[-1], device_id_type=MESH)

    def hear(r):
        pl.semaphore_wait(known.at[r], 2)

    def remote(src, dst, send, recv, device):
        return pltpu.make_async_remote_copy(
            src_ref=src,
            dst_ref=dst,
            send_sem=send,
            recv_sem=recv,
            device_id=device,
            device_id_type=MESH,
        )

    def exchange(peer, count, source, dest, send, recv):
        for step in sorted(range(1, count), key=lambda v: distance(peer, v)):
            *there, device = peer(step)
            remote(source(*there), dest, send, recv, device).start()

    def distance(peer, step):
        return abs(step - {by_pair: 4, by_z: NZ // 2}[peer])

    def await_all(slots, sem):
        pltpu.make_async_copy(slots, slots, sem).wait()

    loads[0].wait()
    loads[1].wait()
    eye8 = iota((8, 8), 0) == iota((8, 8), 1)
    live_col = jnp.sum(
        jnp.where(eye8, jnp.broadcast_to(live[...].astype(F32), (8, 8)), 0.0), axis=1, keepdims=True
    )
    win[REACH] = (tc[...].astype(F32) * live_col[None]).astype(BF16)

    pl.semaphore_wait(barrier, len(peers))
    arriving = {1: [], 3: []}
    for c, part in enumerate(chunks):
        for i, d in enumerate(offsets):
            copy = remote(
                win.at[REACH, part], win.at[REACH - d, part], s_win, r_win.at[i, c], by_window(d)
            )
            copy.start()
            arriving[REACH - d].append(copy)
    for h in range(2):
        exchange(
            by_pair,
            8,
            lambda q: win.at[REACH, pl.ds(4 * (q % 2) + 2 * h, 2)],
            mt.at[h, p_me],
            s_m,
            r_m.at[h],
        )
        mt[h, p_me] = win[REACH, pl.ds(4 * c_me + 2 * h, 2)]

    for c in loads[2:]:
        c.wait()
    new = iota((256, 256), 0)
    old = iota((256, 256), 1)
    perm = jnp.where((new % 8) * 32 + new // 8 == old, 1.0, 0.0).astype(BF16)
    occ_cols = dot(occ[...], perm, ((1,), (1,))).astype(BF16)
    occ_both = dot(perm, occ_cols).astype(BF16)
    atom_row = atoms[...]
    place = iota((64, 64), 0)
    pick = jnp.where((place % 8) * 8 + place // 8 == atom_row, 1.0, 0.0).astype(BF16)
    eye64 = iota((64, 64), 0) == iota((64, 64), 1)
    atom_col = jnp.sum(
        jnp.where(eye64, jnp.broadcast_to(atom_row.astype(F32), (64, 64)), 0.0), axis=1, keepdims=True
    ).astype(jnp.int32)
    spot = iota((64, 64), 1)
    put = jnp.where((spot % 8) * 8 + spot // 8 == atom_col, 1.0, 0.0).astype(BF16)
    held[...] = jnp.broadcast_to(atom_col, (64, 128))
    own_atoms = [
        held[pl.ds(pl.multiple_of((2 * y_me + core) * 8, 8), 8), :] for core in range(2)
    ]
    second = [
        jnp.broadcast_to((v & 7)[None], (OA, 8, 128)).reshape(256, 128) for v in own_atoms
    ]
    wide_col = iota((8, 256), 1)
    firsts = [
        jnp.sum(
            jnp.where(
                iota((8, 256), 0) == wide_col % 8, jnp.concatenate([v, v], axis=1) >> 3, 0
            ).astype(F32),
            axis=0,
            keepdims=True,
        )
        for v in own_atoms
    ]
    column = iota((64, 256), 1)
    first = jnp.where((column // 64) % 2 == 0, firsts[0], firsts[1]).astype(jnp.int32)
    collect = jnp.where(
        jnp.logical_and((atom_col & 7) == (column % 64) // 8, (atom_col >> 3) == first), 1.0, 0.0
    ).astype(BF16)
    wide = jnp.broadcast_to(scr[...].astype(F32)[:, None, :], (8, 8, 40)).reshape(64, 40).astype(BF16)
    same_tile = (iota((64, 64), 0) % 8) == (iota((64, 64), 1) % 8)
    couple = []
    for slot in range(5):
        spread = jnp.where(iota((40, 64), 0) == slot * 8 + iota((40, 64), 1) // 8, 1.0, 0.0)
        block = a_me + slot - REACH
        inside = jnp.logical_and(block >= 0, block < n_aux)
        keep = jnp.logical_and(same_tile, inside)
        couple.append(jnp.where(keep, dot(wide, spread.astype(BF16)), 0.0).astype(BF16))

    tell(0)
    for c, part in enumerate(chunks):
        for i, d in enumerate(offsets):
            arriving[REACH - d][c].wait_recv()
            copy = remote(
                win.at[REACH - d, part],
                win.at[REACH - 2 * d, part],
                s_win,
                r_far.at[i],
                by_window(d),
            )
            copy.start()
    hear(0)
    tell(1)

    def n_half(h):
        await_all(mt.at[h, pl.ds(0, 7)], r_m.at[h])
        for i in range(2):
            form = to_matrix(dot(pick, rows64(mt[h, :, i]).astype(BF16))).astype(BF16)
            forms[2 * h + i] = form
            near[:, 2 * h + i] = dot(occ_cols, form).reshape(NAT, OA, 256).astype(BF16)

    mixed = dot(couple[2], rows64(win[2]).astype(BF16))
    for slot in (1, 3, 0, 4):
        if slot == 0:
            n_half(0)
        if slot in (0, 4):
            await_all(win.at[slot], r_far.at[slot // 4])
        mixed += dot(couple[slot], rows64(win[slot]).astype(BF16))
    vo[...] = mixed.reshape(8, 8, 1024).astype(BF16)
    v_copy = remote(
        vo.at[pl.ds(4 * (1 - c_me), 4)], vt.at[c_me], s_v, r_v, (a_me, y_me * 2 + 1 - c_me)
    )
    v_copy.start()
    vt[c_me] = vo[pl.ds(4 * c_me, 4)]

    n_half(1)

    v_copy.wait_recv()
    v_form = to_matrix(rows64(vt[...]))
    stacked = []
    for core in range(2):
        half = v_form[:, core * 128 : (core + 1) * 128]
        stacked.append(
            jnp.concatenate(
                [jnp.where(second[core] == b, half, 0.0).astype(BF16) for b in range(NAT)], axis=1
            )
        )
    energy = dot(jnp.concatenate(stacked, axis=0), near[...].reshape(1024, 256))
    blocks = [to_tiles(energy[core * 256 : (core + 1) * 256]) for core in range(2)]
    upper = [v.astype(BF16) for v in blocks]
    lower = [(v - u.astype(F32)).astype(BF16) for v, u in zip(blocks, upper)]
    energy_tiles = dot(collect, jnp.concatenate(upper + lower, axis=0))
    for x in range(NX):
        xo[:, x] = energy_tiles[:, x * 256 : (x + 1) * 256].reshape(4, 2, 8, 256).astype(BF16)
    sender = x_me * 8 + p_me
    for step in sorted(range(1, 16), key=lambda v: abs(v % 4 - 2) + abs(v // 4 - 2)):
        y, x, device = by_chip(step)
        remote(xo.at[y, x], xr.at[sender], s_x, r_x, device).start()

    @pl.when(c_me == 0)
    def _():
        remote(xo.at[y_me, x_me], xr.at[sender], s_x, r_x, by_chip(0)[-1]).start()

    @pl.when(c_me == 1)
    def _():
        xr[sender] = xo[y_me, x_me]

    hear(1)
    tell(2)
    left = dot(occ_both, forms[y_me], ((0,), (0,))).astype(BF16)
    z_tiles = dot(put, to_tiles(dot(left, vir[...])).astype(BF16))
    zo[...] = z_tiles.reshape(8, 8, 1024).astype(BF16)
    exchange(by_pair, 8, lambda q: zo.at[q], zt.at[f_me], s_z, r_z)
    zt[f_me] = zo[p_me]

    hear(2)

    @pl.when(c_me == 1)
    def _():
        await_all(xr.at[pl.ds(0, 31)], r_x)
        for core in (1, 0):
            ar[core, z_me] = jnp.sum(xr[:, core].astype(F32), axis=0).astype(BF16)
            own = ar.at[core, z_me]
            exchange(by_z, NZ, lambda z: own, own, s_a.at[core], r_a.at[core])

    await_all(zt.at[pl.ds(0, 7)], r_z)
    z_rows = rows64(zt[...]).astype(BF16)
    chi_total = jnp.zeros((8, 128), F32)
    for slot in range(5):
        terms = dot(z_rows, rows64(win[slot]).astype(BF16), ((1,), (1,)))
        block = a_me + slot - REACH
        inside = jnp.logical_and(block >= 0, block < n_aux)
        keep = jnp.logical_and(same_tile, inside)
        terms = jnp.sum(jnp.where(keep, terms, 0.0).reshape(8, 8, 64), axis=1)
        gather = jnp.where(iota((64, 128), 1) == slot * 8 + iota((64, 128), 0) // 8, 1.0, 0.0)
        chi_total += jnp.dot(terms, gather, precision=lax.Precision.HIGHEST, preferred_element_type=F32)
    chi[p_me] = chi_total * (1.0 / (OA * NAT))
    exchange(by_pair, 8, lambda q: chi.at[p_me], chi.at[p_me], s_c, r_c)

    await_all(win.at[pl.ds(0, 4)], s_win)
    await_all(mt.at[:, pl.ds(0, 7)], s_m)
    v_copy.wait_send()
    await_all(zt.at[pl.ds(0, 7)], s_z)
    @pl.when(c_me == 0)
    def _():
        await_all(xr.at[pl.ds(0, 16)], s_x)

    @pl.when(c_me == 1)
    def _():
        await_all(xr.at[pl.ds(0, 15)], s_x)

    scale = -1.0 / math.sqrt(n_aux * 8 * NAT * OA * NAT)

    @pl.when(c_me == 1)
    def _():
        for core in (1, 0):
            await_all(ar.at[core, pl.ds(0, NZ - 1)], r_a.at[core])
            both[core] = jnp.sum(ar[core].astype(F32), axis=0) * scale
            for step in (2, 1, 3):
                there = (by_x(step)[-1][0], y_me * 2 + core)
                remote(both.at[core], fin.at[x_me], s_f, r_f, there).start()
        remote(both.at[0], fin.at[x_me], s_f, r_f, (a_me, y_me * 2)).start()
        fin[x_me] = both[1]

    await_all(chi.at[pl.ds(0, 7)], r_c)
    turned = pltpu.roll(jnp.sum(chi[...], axis=0), lax.rem(128 - 5 * p_me, 128), 1)
    pol_ref[...] = turned[:, :5]
    await_all(chi.at[pl.ds(0, 7)], s_c)

    @pl.when(c_me == 1)
    def _():
        for core in range(2):
            await_all(ar.at[core, pl.ds(0, NZ - 1)], s_a.at[core])
        await_all(fin.at[pl.ds(0, NX - 1)], r_f)

    @pl.when(c_me == 0)
    def _():
        await_all(fin, r_f)

    for x in range(NX):
        self_ref[:, x * 256 : (x + 1) * 256] = fin[x]

    @pl.when(c_me == 1)
    def _():
        await_all(xr.at[pl.ds(0, 7)], s_f)


def solution(mesh):
    n_aux, n_pair = mesh.shape["aux"], mesh.shape["pair"]

    def per_device(three_center, tile_live, pair_atoms, green_occ, green_vir, screened):
        tiles = pltpu.VMEM((8, 8, 1024), BF16)
        return pl.pallas_call(
            functools.partial(kernel, n_aux, n_pair),
            out_shape=(
                jax.ShapeDtypeStruct((8, 5), F32),
                jax.ShapeDtypeStruct((8, 1024), F32),
            ),
            in_specs=[pl.BlockSpec(memory_space=pl.ANY)] * 6,
            out_specs=[pl.BlockSpec(memory_space=pltpu.VMEM)] * 2,
            scratch_shapes=[
                tiles,
                pltpu.VMEM((1, 8), jnp.int32),
                pltpu.VMEM((1, 64), jnp.int32),
                pltpu.VMEM((256, 256), BF16),
                pltpu.VMEM((256, 256), BF16),
                pltpu.VMEM((8, 40), BF16),
                pltpu.VMEM((5, 8, 8, 1024), BF16),
                pltpu.VMEM((2, 8, 2, 8, 1024), BF16),
                *[tiles] * 3,
                pltpu.VMEM((2, 4, 8, 1024), BF16),
                pltpu.VMEM((64, 128), jnp.int32),
                pltpu.VMEM((4, 256, 256), BF16),
                pltpu.VMEM((NAT, 4, OA, 256), BF16),
                pltpu.VMEM((4, NX, 2, 8, 256), BF16),
                pltpu.VMEM((32, 2, 8, 256), BF16),
                pltpu.VMEM((8, 8, 128), F32),
                pltpu.VMEM((2, NZ, 8, 256), BF16),
                pltpu.VMEM((2, 8, 256), F32),
                pltpu.VMEM((NX, 8, 256), F32),
                pltpu.SemaphoreType.DMA((6,)),
                pltpu.SemaphoreType.DMA(()),
                pltpu.SemaphoreType.DMA((2, 4)),
                pltpu.SemaphoreType.DMA((2,)),
                pltpu.SemaphoreType.DMA(()),
                pltpu.SemaphoreType.DMA((2,)),
                *[pltpu.SemaphoreType.DMA(())] * 8,
                *[pltpu.SemaphoreType.DMA((2,))] * 2,
                *[pltpu.SemaphoreType.DMA(())] * 2,
                pltpu.SemaphoreType.REGULAR((3,)),
            ],
            compiler_params=pltpu.CompilerParams(
                collective_id=0, has_side_effects=True, vmem_limit_bytes=40 << 20
            ),
        )(
            *(
                pltpu.with_memory_space_constraint(v, pltpu.HBM)
                for v in (
                    three_center,
                    tile_live,
                    pair_atoms.reshape(1, 64),
                    green_occ,
                    green_vir,
                    screened,
                )
            )
        )

    placed = (P("aux", "pair", None), P("aux", "pair"), P(), P(), P(), P("aux", None))
    return jax.shard_map(
        per_device,
        mesh=mesh,
        in_specs=placed,
        out_specs=(P("aux", "pair"), P("pair", None)),
        check_vma=False,
    )
```

```python
import functools
import math

import jax
import jax.numpy as jnp
from jax import lax
from jax.experimental import pallas as pl
from jax.experimental.pallas import tpu as pltpu
from jax.sharding import PartitionSpec as P

MESH = pl.DeviceIdType.MESH
OA = 32
NAT = 8
REACH = 2
NX = 4
NZ = 16
F32 = jnp.float32
BF16 = jnp.bfloat16


def dot(a, b, dims=((1,), (0,))):
    return lax.dot_general(a, b, (dims, ((), ())), preferred_element_type=F32)


def iota(shape, dim):
    return lax.broadcasted_iota(jnp.int32, shape, dim)


def exchange_groups(parts):
    x0, x1, x2, x3 = parts
    lane = iota(x0.shape, 1)
    low = lane < 64
    even = (lane & 32) == 0
    y0 = jnp.where(low, x0, pltpu.roll(x2, 64, 1))
    y2 = jnp.where(low, pltpu.roll(x0, 64, 1), x2)
    y1 = jnp.where(low, x1, pltpu.roll(x3, 64, 1))
    y3 = jnp.where(low, pltpu.roll(x1, 64, 1), x3)
    z0 = jnp.where(even, y0, pltpu.roll(y1, 32, 1))
    z1 = jnp.where(even, pltpu.roll(y0, 96, 1), y1)
    z2 = jnp.where(even, y2, pltpu.roll(y3, 32, 1))
    z3 = jnp.where(even, pltpu.roll(y2, 96, 1), y3)
    return z0, z1, z2, z3


def to_matrix(tiles):
    cols = [tiles[:, g * 128 : (g + 1) * 128].reshape(2, 4, 8, 128) for g in range(8)]
    parts = [
        jnp.concatenate([c[:, bl] for c in cols], axis=0).reshape(128, 128) for bl in range(4)
    ]
    out = [z.reshape(8, 2, 8, 128) for z in exchange_groups(parts)]
    halves = [
        jnp.stack([z[:, bh] for z in out], axis=1).reshape(256, 128) for bh in range(2)
    ]
    return jnp.concatenate(halves, axis=1)


def to_tiles(matrix):
    halves = [matrix[:, bh * 128 : (bh + 1) * 128].reshape(8, 4, 8, 128) for bh in range(2)]
    parts = [
        jnp.stack([h[:, r] for h in halves], axis=1).reshape(128, 128) for r in range(4)
    ]
    out = [z.reshape(8, 2, 8, 128) for z in exchange_groups(parts)]
    cols = [
        jnp.stack([z[g] for z in out], axis=1).reshape(64, 128) for g in range(8)
    ]
    return jnp.concatenate(cols, axis=1)


def rows64(value):
    return value.astype(F32).reshape(64, value.shape[-1])


def kernel(
    n_aux,
    n_pair,
    tc_hbm,
    live_hbm,
    atoms_hbm,
    occ_hbm,
    vir_hbm,
    scr_hbm,
    pol_ref,
    self_ref,
    tc,
    live,
    atoms,
    occ,
    vir,
    scr,
    win,
    mt,
    zo,
    zt,
    vo,
    vt,
    held,
    forms,
    near,
    xo,
    xr,
    chi,
    ar,
    both,
    fin,
    in_sem,
    s_near,
    r_near,
    s_far,
    r_far,
    s_m,
    r_m,
    s_z,
    r_z,
    s_v,
    r_v,
    s_x,
    r_x,
    s_c,
    r_c,
    s_a,
    r_a,
    s_f,
    r_f,
    known,
):
    a_me = lax.axis_index("aux")
    p_me = lax.axis_index("pair")
    x_me, z_me = a_me // NZ, a_me % NZ
    y_me, c_me = p_me // 2, p_me % 2
    f_me = c_me * 4 + y_me

    def by_pair(step):
        q = lax.rem(p_me + step, n_pair)
        return q, (a_me, q)

    def by_chip(step):
        x = lax.rem(x_me + step // 4, NX)
        y = lax.rem(y_me + step % 4, 4)
        return y, x, (x * NZ + z_me, y * 2 + 1)

    def by_z(step):
        z = lax.rem(z_me + step, NZ)
        return z, (x_me * NZ + z, p_me)

    def by_x(step):
        x = lax.rem(x_me + step, NX)
        return x, (x * NZ + z_me, p_me)

    offsets = (1, -1)
    chunks = [pl.ds(2 * c, 2) for c in range(4)]

    def inside(block):
        return jnp.logical_and(block >= 0, block < n_aux)

    def by_window(d):
        return (lax.rem(a_me + d + n_aux, n_aux), p_me)

    barrier = pltpu.get_barrier_semaphore()
    peers = [by_window(d) for d in offsets]
    peers += [by_x(step)[-1] for step in (2, 1, 3)]
    peers += [by_pair(step)[-1] for step in range(1, 8)]
    peers += [by_z(step)[-1] for step in (1, NZ - 1)]
    for device in peers:
        pl.semaphore_signal(barrier, inc=1, device_id=device, device_id_type=MESH)

    loads = [
        pltpu.make_async_copy(src, dst, in_sem.at[i])
        for i, (src, dst) in enumerate(
            (
                (tc_hbm, tc),
                (live_hbm, live),
                (atoms_hbm, atoms),
                (occ_hbm, occ),
                (vir_hbm, vir),
                (scr_hbm, scr),
            )
        )
    ]
    for c in loads:
        c.start()

    def tell(r):
        for step in (1 << r, NZ - (1 << r)):
            pl.semaphore_signal(known.at[r], inc=1, device_id=by_z(step)[-1], device_id_type=MESH)

    def hear(r):
        pl.semaphore_wait(known.at[r], 2)

    def remote(src, dst, send, recv, device):
        return pltpu.make_async_remote_copy(
            src_ref=src,
            dst_ref=dst,
            send_sem=send,
            recv_sem=recv,
            device_id=device,
            device_id_type=MESH,
        )

    def exchange(peer, count, source, dest, send, recv):
        for step in sorted(range(1, count), key=lambda v: distance(peer, v)):
            *there, device = peer(step)
            remote(source(*there), dest, send, recv, device).start()

    def distance(peer, step):
        return abs(step - {by_pair: 4, by_z: NZ // 2}[peer])

    def await_all(slots, sem):
        pltpu.make_async_copy(slots, slots, sem).wait()

    loads[0].wait()
    loads[1].wait()
    eye8 = iota((8, 8), 0) == iota((8, 8), 1)
    live_col = jnp.sum(
        jnp.where(eye8, jnp.broadcast_to(live[...].astype(F32), (8, 8)), 0.0), axis=1, keepdims=True
    )
    win[REACH] = (tc[...].astype(F32) * live_col[None]).astype(BF16)

    for slot in (0, 1, 3, 4):

        @pl.when(jnp.logical_not(inside(a_me + slot - REACH)))
        def _():
            win[slot] = jnp.zeros((8, 8, 1024), BF16)

    pl.semaphore_wait(barrier, len(peers))
    def near_copy(i, c):
        slot = REACH - offsets[i]
        return remote(
            win.at[REACH, chunks[c]],
            win.at[slot, chunks[c]],
            s_near.at[i],
            r_near.at[i, c],
            by_window(offsets[i]),
        )

    for c in range(len(chunks)):
        for i, d in enumerate(offsets):

            @pl.when(inside(a_me + d))
            def _():
                near_copy(i, c).start()

    for h in range(2):
        exchange(
            by_pair,
            8,
            lambda q: win.at[REACH, pl.ds(4 * (q % 2) + 2 * h, 2)],
            mt.at[h, p_me],
            s_m,
            r_m.at[h],
        )
        mt[h, p_me] = win[REACH, pl.ds(4 * c_me + 2 * h, 2)]

    for c in loads[2:]:
        c.wait()
    new = iota((256, 256), 0)
    old = iota((256, 256), 1)
    perm = jnp.where((new % 8) * 32 + new // 8 == old, 1.0, 0.0).astype(BF16)
    occ_cols = dot(occ[...], perm, ((1,), (1,))).astype(BF16)
    occ_both = dot(perm, occ_cols).astype(BF16)
    atom_row = atoms[...]
    place = iota((64, 64), 0)
    pick = jnp.where((place % 8) * 8 + place // 8 == atom_row, 1.0, 0.0).astype(BF16)
    eye64 = iota((64, 64), 0) == iota((64, 64), 1)
    atom_col = jnp.sum(
        jnp.where(eye64, jnp.broadcast_to(atom_row.astype(F32), (64, 64)), 0.0), axis=1, keepdims=True
    ).astype(jnp.int32)
    spot = iota((64, 64), 1)
    put = jnp.where((spot % 8) * 8 + spot // 8 == atom_col, 1.0, 0.0).astype(BF16)
    held[...] = jnp.broadcast_to(atom_col, (64, 128))
    own_atoms = [
        held[pl.ds(pl.multiple_of((2 * y_me + core) * 8, 8), 8), :] for core in range(2)
    ]
    second = [
        jnp.broadcast_to((v & 7)[None], (OA, 8, 128)).reshape(256, 128) for v in own_atoms
    ]
    wide_col = iota((8, 256), 1)
    firsts = [
        jnp.sum(
            jnp.where(
                iota((8, 256), 0) == wide_col % 8, jnp.concatenate([v, v], axis=1) >> 3, 0
            ).astype(F32),
            axis=0,
            keepdims=True,
        )
        for v in own_atoms
    ]
    column = iota((64, 256), 1)
    first = jnp.where((column // 64) % 2 == 0, firsts[0], firsts[1]).astype(jnp.int32)
    collect = jnp.where(
        jnp.logical_and((atom_col & 7) == (column % 64) // 8, (atom_col >> 3) == first), 1.0, 0.0
    ).astype(BF16)
    wide = jnp.broadcast_to(scr[...].astype(F32)[:, None, :], (8, 8, 40)).reshape(64, 40).astype(BF16)
    same_tile = (iota((64, 64), 0) % 8) == (iota((64, 64), 1) % 8)
    couple = []
    for slot in range(5):
        spread = jnp.where(iota((40, 64), 0) == slot * 8 + iota((40, 64), 1) // 8, 1.0, 0.0)
        keep = jnp.logical_and(same_tile, inside(a_me + slot - REACH))
        couple.append(jnp.where(keep, dot(wide, spread.astype(BF16)), 0.0).astype(BF16))

    tell(0)
    for c, part in enumerate(chunks):
        for i, d in enumerate(offsets):

            @pl.when(inside(a_me - d))
            def _():
                near_copy(i, c).wait_recv()

            @pl.when(jnp.logical_and(inside(a_me - d), inside(a_me + d)))
            def _():
                remote(
                    win.at[REACH - d, part],
                    win.at[REACH - 2 * d, part],
                    s_far.at[i],
                    r_far.at[i],
                    by_window(d),
                ).start()

    hear(0)
    tell(1)

    def n_half(h):
        await_all(mt.at[h, pl.ds(0, 7)], r_m.at[h])
        for i in range(2):
            form = to_matrix(dot(pick, rows64(mt[h, :, i]).astype(BF16))).astype(BF16)
            forms[2 * h + i] = form
            near[:, 2 * h + i] = dot(occ_cols, form).reshape(NAT, OA, 256).astype(BF16)

    mixed = dot(couple[2], rows64(win[2]).astype(BF16))
    for slot in (1, 3, 0, 4):
        if slot == 0:
            n_half(0)
        if slot in (0, 4):

            @pl.when(inside(a_me + slot - REACH))
            def _():
                await_all(win.at[slot], r_far.at[slot // 4])

        mixed += dot(couple[slot], rows64(win[slot]).astype(BF16))
    vo[...] = mixed.reshape(8, 8, 1024).astype(BF16)
    v_copy = remote(
        vo.at[pl.ds(4 * (1 - c_me), 4)], vt.at[c_me], s_v, r_v, (a_me, y_me * 2 + 1 - c_me)
    )
    v_copy.start()
    vt[c_me] = vo[pl.ds(4 * c_me, 4)]

    n_half(1)

    v_copy.wait_recv()
    v_form = to_matrix(rows64(vt[...]))
    stacked = []
    for core in range(2):
        half = v_form[:, core * 128 : (core + 1) * 128]
        stacked.append(
            jnp.concatenate(
                [jnp.where(second[core] == b, half, 0.0).astype(BF16) for b in range(NAT)], axis=1
            )
        )
    energy = dot(jnp.concatenate(stacked, axis=0), near[...].reshape(1024, 256))
    blocks = [to_tiles(energy[core * 256 : (core + 1) * 256]) for core in range(2)]
    upper = [v.astype(BF16) for v in blocks]
    lower = [(v - u.astype(F32)).astype(BF16) for v, u in zip(blocks, upper)]
    energy_tiles = dot(collect, jnp.concatenate(upper + lower, axis=0))
    for x in range(NX):
        xo[:, x] = energy_tiles[:, x * 256 : (x + 1) * 256].reshape(4, 2, 8, 256).astype(BF16)
    sender = x_me * 8 + p_me
    for step in sorted(range(1, 16), key=lambda v: abs(v % 4 - 2) + abs(v // 4 - 2)):
        y, x, device = by_chip(step)
        remote(xo.at[y, x], xr.at[sender], s_x, r_x, device).start()

    @pl.when(c_me == 0)
    def _():
        remote(xo.at[y_me, x_me], xr.at[sender], s_x, r_x, by_chip(0)[-1]).start()

    @pl.when(c_me == 1)
    def _():
        xr[sender] = xo[y_me, x_me]

    hear(1)
    tell(2)
    left = dot(occ_both, forms[y_me], ((0,), (0,))).astype(BF16)
    z_tiles = dot(put, to_tiles(dot(left, vir[...])).astype(BF16))
    zo[...] = z_tiles.reshape(8, 8, 1024).astype(BF16)
    exchange(by_pair, 8, lambda q: zo.at[q], zt.at[f_me], s_z, r_z)
    zt[f_me] = zo[p_me]

    hear(2)

    @pl.when(c_me == 1)
    def _():
        await_all(xr.at[pl.ds(0, 31)], r_x)
        for core in (1, 0):
            ar[core, z_me] = jnp.sum(xr[:, core].astype(F32), axis=0).astype(BF16)
            own = ar.at[core, z_me]
            exchange(by_z, NZ, lambda z: own, own, s_a.at[core], r_a.at[core])

    await_all(zt.at[pl.ds(0, 7)], r_z)
    z_rows = rows64(zt[...]).astype(BF16)
    chi_total = jnp.zeros((8, 128), F32)
    for slot in range(5):
        terms = dot(z_rows, rows64(win[slot]).astype(BF16), ((1,), (1,)))
        keep = jnp.logical_and(same_tile, inside(a_me + slot - REACH))
        terms = jnp.sum(jnp.where(keep, terms, 0.0).reshape(8, 8, 64), axis=1)
        gather = jnp.where(iota((64, 128), 1) == slot * 8 + iota((64, 128), 0) // 8, 1.0, 0.0)
        chi_total += jnp.dot(terms, gather, precision=lax.Precision.HIGHEST, preferred_element_type=F32)
    chi[p_me] = chi_total * (1.0 / (OA * NAT))
    exchange(by_pair, 8, lambda q: chi.at[p_me], chi.at[p_me], s_c, r_c)

    for i, d in enumerate(offsets):

        @pl.when(inside(a_me + d))
        def _():
            await_all(win.at[REACH], s_near.at[i])

        @pl.when(jnp.logical_and(inside(a_me - d), inside(a_me + d)))
        def _():
            await_all(win.at[REACH], s_far.at[i])

    await_all(mt.at[:, pl.ds(0, 7)], s_m)
    v_copy.wait_send()
    await_all(zt.at[pl.ds(0, 7)], s_z)
    @pl.when(c_me == 0)
    def _():
        await_all(xr.at[pl.ds(0, 16)], s_x)

    @pl.when(c_me == 1)
    def _():
        await_all(xr.at[pl.ds(0, 15)], s_x)

    scale = -1.0 / math.sqrt(n_aux * 8 * NAT * OA * NAT)

    @pl.when(c_me == 1)
    def _():
        for core in (1, 0):
            await_all(ar.at[core, pl.ds(0, NZ - 1)], r_a.at[core])
            both[core] = jnp.sum(ar[core].astype(F32), axis=0) * scale
            for step in (2, 1, 3):
                there = (by_x(step)[-1][0], y_me * 2 + core)
                remote(both.at[core], fin.at[x_me], s_f, r_f, there).start()
        remote(both.at[0], fin.at[x_me], s_f, r_f, (a_me, y_me * 2)).start()
        fin[x_me] = both[1]

    await_all(chi.at[pl.ds(0, 7)], r_c)
    turned = pltpu.roll(jnp.sum(chi[...], axis=0), lax.rem(128 - 5 * p_me, 128), 1)
    pol_ref[...] = turned[:, :5]
    await_all(chi.at[pl.ds(0, 7)], s_c)

    @pl.when(c_me == 1)
    def _():
        for core in range(2):
            await_all(ar.at[core, pl.ds(0, NZ - 1)], s_a.at[core])
        await_all(fin.at[pl.ds(0, NX - 1)], r_f)

    @pl.when(c_me == 0)
    def _():
        await_all(fin, r_f)

    for x in range(NX):
        self_ref[:, x * 256 : (x + 1) * 256] = fin[x]

    @pl.when(c_me == 1)
    def _():
        await_all(xr.at[pl.ds(0, 7)], s_f)


def solution(mesh):
    n_aux, n_pair = mesh.shape["aux"], mesh.shape["pair"]

    def per_device(three_center, tile_live, pair_atoms, green_occ, green_vir, screened):
        tiles = pltpu.VMEM((8, 8, 1024), BF16)
        return pl.pallas_call(
            functools.partial(kernel, n_aux, n_pair),
            out_shape=(
                jax.ShapeDtypeStruct((8, 5), F32),
                jax.ShapeDtypeStruct((8, 1024), F32),
            ),
            in_specs=[pl.BlockSpec(memory_space=pl.ANY)] * 6,
            out_specs=[pl.BlockSpec(memory_space=pltpu.VMEM)] * 2,
            scratch_shapes=[
                tiles,
                pltpu.VMEM((1, 8), jnp.int32),
                pltpu.VMEM((1, 64), jnp.int32),
                pltpu.VMEM((256, 256), BF16),
                pltpu.VMEM((256, 256), BF16),
                pltpu.VMEM((8, 40), BF16),
                pltpu.VMEM((5, 8, 8, 1024), BF16),
                pltpu.VMEM((2, 8, 2, 8, 1024), BF16),
                *[tiles] * 3,
                pltpu.VMEM((2, 4, 8, 1024), BF16),
                pltpu.VMEM((64, 128), jnp.int32),
                pltpu.VMEM((4, 256, 256), BF16),
                pltpu.VMEM((NAT, 4, OA, 256), BF16),
                pltpu.VMEM((4, NX, 2, 8, 256), BF16),
                pltpu.VMEM((32, 2, 8, 256), BF16),
                pltpu.VMEM((8, 8, 128), F32),
                pltpu.VMEM((2, NZ, 8, 256), BF16),
                pltpu.VMEM((2, 8, 256), F32),
                pltpu.VMEM((NX, 8, 256), F32),
                pltpu.SemaphoreType.DMA((6,)),
                pltpu.SemaphoreType.DMA((2,)),
                pltpu.SemaphoreType.DMA((2, 4)),
                *[pltpu.SemaphoreType.DMA((2,))] * 2,
                pltpu.SemaphoreType.DMA(()),
                pltpu.SemaphoreType.DMA((2,)),
                *[pltpu.SemaphoreType.DMA(())] * 8,
                *[pltpu.SemaphoreType.DMA((2,))] * 2,
                *[pltpu.SemaphoreType.DMA(())] * 2,
                pltpu.SemaphoreType.REGULAR((3,)),
            ],
            compiler_params=pltpu.CompilerParams(
                collective_id=0, has_side_effects=True, vmem_limit_bytes=40 << 20
            ),
        )(
            *(
                pltpu.with_memory_space_constraint(v, pltpu.HBM)
                for v in (
                    three_center,
                    tile_live,
                    pair_atoms.reshape(1, 64),
                    green_occ,
                    green_vir,
                    screened,
                )
            )
        )

    placed = (P("aux", "pair", None), P("aux", "pair"), P(), P(), P(), P("aux", None))
    return jax.shard_map(
        per_device,
        mesh=mesh,
        in_specs=placed,
        out_specs=(P("aux", "pair"), P("pair", None)),
        check_vma=False,
    )
```
